32 devices in a mesh: fsdp: 8 (over z, x), ctx: 4 (over y, core).
Axes of the slice: x: 2, y: 2, z: 4, core: 2. Of those that a mesh axis runs over, the one named last changes fastest.
Arguments:
- tokens: bfloat16 [8, 512, 4096], P('fsdp', 'ctx'), may hold values from -6 to 6
- norm_gain: float32 [4096], replicated, may hold values from 0.5 to 1.5
- w_in: bfloat16 [4096, 3, 4096], P(None, None, 'fsdp'), may hold values from -0.09375 to 0.09375
- taps: float32 [3, 3, 4096], P(None, None, 'fsdp'), may hold values from -3 to 3
- decay_rate: float32 [16, 4096], P(None, 'fsdp'), may hold values from 0 to 0.0334, as said below
- residues: float32 [16, 4096], P(None, 'fsdp'), may hold values from -0.12 to 0.12
- skip_gain: float32 [4096], P('fsdp'), may hold values from -4 to 4
- w_out: bfloat16 [4096, 4096], P('fsdp'), may hold values from -0.09375 to 0.09375
Outputs:
- mixed: bfloat16 [8, 512, 4096], P('fsdp', 'ctx')
The draws below stay inside these ranges and needn't reach their ends.
Inputs may be any that keep to these rules, and one draw needn't show every extreme that they name: `decay_rate`: positive decay rates of the poles, at most 1/30.
All inputs are finite; a program needn't handle non-finite values.
Results may differ from the reference program's by a relative error of at most 0.024.
Values may be sent and summed in bfloat16 or wider, within the bound.
A program may use at most 192 MiB of HBM per device.

```python
import math
import jax
import jax.numpy as jnp
from jax import lax

D = 4096
NP = 16
TAPS = 3
TOK_DEV = 128
SEQ = 512
SEQS = 8
N_FSDP = 8
N_CTX = 4


def draw_decay_rate(key, part):
    key = jax.random.fold_in(key, 11)
    lower = math.log(0.3 / SEQ)
    upper = math.log(1.0 / 30.0)
    exponent = jax.random.uniform(key, (NP, D), jnp.float32, lower, upper)
    return jnp.exp(exponent)


def level_of(own_key, shape, cuts, least, largest):
    gain, own = 1.0, jax.random.fold_in(own_key, 6)
    for dim, shards_of in cuts:
        steps = jnp.exp(jax.random.uniform(jax.random.fold_in(own, dim), (shards_of,), jnp.float32, least / len(cuts), largest / len(cuts)))
        gain = gain * jnp.repeat(steps, shape[dim] // shards_of).reshape([-1 if axis == dim else 1 for axis in range(len(shape))])
    return gain


def bell_draw(stream_key, shape, spread, bound, pieces=(), held_as=jnp.bfloat16):
    array = jax.random.normal(stream_key, shape, jnp.float32) * spread
    if len(pieces) > 0:
        array = level_of(stream_key, shape, pieces, -0.22, 0.18) * array
    return jnp.clip(array, min=-bound, max=bound).astype(held_as)


def setup_inputs(seed: int = 0) -> dict:
    key_of = jax.random.split(jax.random.key(seed), 9)
    return {
        "tokens": bell_draw(key_of[0], (SEQS, SEQ, D), 1.0, 6.0, ((0, 8), (1, 4))),
        "norm_gain": jnp.clip(1.0 + 0.1 * jax.random.normal(key_of[1], (D,), jnp.float32), 0.5, 1.5),
        "w_in": bell_draw(key_of[2], (D, 3, D), D ** -0.5, 0.09375, ((2, 8),)),
        "taps": bell_draw(key_of[3], (TAPS, 3, D), 0.6, 3.0, ((2, 8),), jnp.float32),
        "decay_rate": draw_decay_rate(jax.random.fold_in(key_of[8], 71), 0),
        "residues": bell_draw(key_of[5], (NP, D), 0.02, 0.12, ((1, 8),), jnp.float32),
        "skip_gain": bell_draw(key_of[6], (D,), 1.0, 4.0, ((0, 8),), jnp.float32),
        "w_out": bell_draw(key_of[7], (D, D), D ** -0.5, 0.09375, ((0, 8),)),
    }


def reference(tokens, norm_gain, w_in, taps, decay_rate, residues, skip_gain, w_out):
    high = lax.Precision.HIGHEST
    values = tokens.astype(jnp.float32)
    inverse_rms = lax.rsqrt(lax.optimization_barrier(jnp.mean(values * values, axis=-1, keepdims=True)) + 1e-06)
    normed = (values * inverse_rms * norm_gain).astype(jnp.bfloat16)
    features = jnp.dot(normed.reshape(SEQS * SEQ, D), w_in.reshape(D, 3 * D), preferred_element_type=jnp.float32)
    features = features.astype(jnp.bfloat16).reshape(SEQS, SEQ, 3, D).astype(jnp.float32)
    padded = jnp.pad(features, ((0, 0), (2, 0), (0, 0), (0, 0)))
    filtered = taps[0] * padded[:, 2:] + taps[1] * padded[:, 1:-1] + taps[2] * padded[:, :-2]
    query_part = filtered[:, :, 0]
    product = filtered[:, :, 1] * filtered[:, :, 2]
    offsets = jnp.arange(TOK_DEV, dtype=jnp.float32)
    powers = jnp.exp(-decay_rate[:, None, :] * offsets[None, :, None])
    kernel = lax.optimization_barrier(jnp.sum(residues[:, None, :] * powers, axis=0))
    positions = jnp.arange(TOK_DEV, dtype=jnp.int32)
    lag_steps = positions[:, None] - positions[None, :]
    toeplitz = jnp.where((lag_steps >= 0)[:, :, None], kernel[jnp.maximum(lag_steps, 0)], jnp.float32(0.0))
    end_pow = jnp.exp(-decay_rate[:, None, :] * (TOK_DEV - 1 - offsets)[None, :, None])
    enter = residues[:, None, :] * jnp.exp(-decay_rate[:, None, :] * (offsets + 1.0)[None, :, None])
    decay_all = jnp.exp(-decay_rate * TOK_DEV)
    blocks = product.reshape(SEQS, N_CTX, TOK_DEV, D).transpose(1, 0, 2, 3)

    def advance(carried, block_rows):
        inside = jnp.einsum('tsc,gsc->gtc', toeplitz, block_rows, precision=high)
        entering = jnp.einsum('ntc,gnc->gtc', enter, carried, precision=high)
        summary = jnp.einsum('nsc,gsc->gnc', end_pow, block_rows, precision=high)
        return (decay_all * carried + summary, inside + entering)
    _, conv = lax.scan(advance, jnp.zeros((SEQS, NP, D), jnp.float32), blocks)
    conv = conv.transpose(1, 0, 2, 3).reshape(SEQS, SEQ, D)
    response = skip_gain * product + conv
    gated = (query_part * response).astype(jnp.bfloat16)
    flat_rows = gated.reshape(SEQS * SEQ, D)
    block_width = D // N_FSDP

    def add_part(running, which):
        first = (which * block_width).astype(jnp.int32)
        columns = lax.dynamic_slice_in_dim(flat_rows, first, block_width, 1)
        weights = lax.dynamic_slice_in_dim(w_out, first, block_width, 0)
        partial_value = jnp.dot(columns, weights, preferred_element_type=jnp.float32).astype(jnp.bfloat16)
        partial_value = lax.optimization_barrier(partial_value)
        return (running + partial_value.astype(jnp.float32), None)
    running, _ = lax.scan(add_part, jnp.zeros((SEQS * SEQ, D), jnp.float32), jnp.arange(N_FSDP, dtype=jnp.int32))
    result = values.reshape(SEQS * SEQ, D) + running
    return result.astype(jnp.bfloat16).reshape(SEQS, SEQ, D)
```

```python
import jax
import jax.numpy as jnp
from jax import lax
from jax.experimental import pallas as pl
from jax.experimental.pallas import tpu as pltpu
from jax.sharding import PartitionSpec as P


def from_behind(value, axis, steps):
    count = lax.axis_size(axis)
    first, last = (max(0, -steps), min(count, count - steps))
    return lax.ppermute(value, axis, [(source, source + steps) for source in range(first, last)])


LANES = 128


def summary_kernel(decay_ref, product_ref, out_ref):
    poles, groups, lanes = out_ref.shape
    decay = jnp.broadcast_to(jnp.exp(-decay_ref[...])[:, None, :], (poles, groups, lanes))

    def step(t, state):
        return decay * state + product_ref[t][None]

    out_ref[...] = lax.fori_loop(0, product_ref.shape[0], step, jnp.zeros(out_ref.shape, jnp.float32))


def filter_kernel(decay_ref, residues_ref, skip_ref, product_ref, query_ref, incoming_ref, out_ref):
    poles, groups, lanes = incoming_ref.shape
    decay = jnp.broadcast_to(jnp.exp(-decay_ref[...])[:, None, :], (poles, groups, lanes))
    residues = residues_ref[...][:, None, :]
    skip = skip_ref[...]

    def step(t, state):
        product = product_ref[t]
        state = decay * state + product[None]
        out_ref[t] = query_ref[t] * (skip * product + jnp.sum(residues * state, axis=0))
        return state

    lax.fori_loop(0, product_ref.shape[0], step, incoming_ref[...])


def shards(tokens, norm_gain, w_in, taps, decay_rate, residues, skip_gain, w_out):
    values = tokens.astype(jnp.float32)
    inverse_rms = lax.rsqrt(jnp.mean(values * values, axis=-1, keepdims=True) + 1e-06)
    normed = (values * inverse_rms * norm_gain).astype(jnp.bfloat16)
    model_width = w_in.shape[0]
    channels = w_in.shape[2]
    w_flat = w_in.reshape(model_width, 3 * channels)
    features = jnp.einsum(
        "gtd,de->gte",
        lax.all_gather(normed, "fsdp", axis=0, tiled=True),
        w_flat,
        preferred_element_type=jnp.float32,
    ).astype(jnp.bfloat16)
    groups = features.shape[0]
    length = features.shape[1]
    poles = decay_rate.shape[0]
    edge_rows = from_behind(features[:, length - 2 :], "ctx", 1)
    extended = jnp.concatenate([edge_rows, features], axis=1).transpose(1, 0, 2).astype(jnp.float32)
    tap_rows = taps.reshape(taps.shape[0], 3 * channels)
    filtered = tap_rows[0] * extended[2:] + tap_rows[1] * extended[1:-1] + tap_rows[2] * extended[:-2]
    query_part = filtered[:, :, :channels]
    product = filtered[:, :, channels : 2 * channels] * filtered[:, :, 2 * channels :]
    pole_spec = pl.BlockSpec((poles, LANES), lambda c: (0, c))
    state_spec = pl.BlockSpec((poles, groups, LANES), lambda c: (0, 0, c))
    rows_spec = pl.BlockSpec((length, groups, LANES), lambda c: (0, 0, c))
    summary = pl.pallas_call(
        summary_kernel,
        grid=(channels // LANES,),
        in_specs=[pole_spec, rows_spec],
        out_specs=state_spec,
        out_shape=jax.ShapeDtypeStruct((poles, groups, channels), jnp.float32),
    )(decay_rate, product)
    decay_all = jnp.exp(-decay_rate * length)[:, None, :]
    incoming = jnp.zeros_like(summary)
    for hop_step in range(lax.axis_size("ctx") - 1):
        incoming = from_behind(
            (decay_all * incoming + summary).astype(jnp.bfloat16), "ctx", 1
        ).astype(jnp.float32)
    gated = pl.pallas_call(
        filter_kernel,
        grid=(channels // LANES,),
        in_specs=[pole_spec, pole_spec, pl.BlockSpec((1, LANES), lambda c: (0, c)), rows_spec, rows_spec, state_spec],
        out_specs=rows_spec,
        out_shape=jax.ShapeDtypeStruct((length, groups, channels), jnp.float32),
    )(decay_rate, residues, skip_gain[None], product, query_part, incoming)
    gated = gated.astype(jnp.bfloat16).transpose(1, 0, 2).reshape(groups * length, channels)
    summed = lax.psum_scatter(
        jnp.dot(gated, w_out, preferred_element_type=jnp.float32).astype(jnp.bfloat16),
        "fsdp",
        scatter_dimension=0,
        tiled=True,
    ).astype(jnp.float32)
    return (values[0] + summed).astype(jnp.bfloat16)[None]


def solution(mesh):
    in_specs = (
        P("fsdp", "ctx", None),
        P(),
        P(None, None, "fsdp"),
        P(None, None, "fsdp"),
        P(None, "fsdp"),
        P(None, "fsdp"),
        P("fsdp"),
        P("fsdp", None),
    )
    out_specs = P("fsdp", "ctx", None)
    return jax.shard_map(shards, mesh=mesh, in_specs=in_specs, out_specs=out_specs, check_vma=False)
```

```python
import functools

import jax
import jax.numpy as jnp
from jax import lax
from jax.experimental import pallas as pl
from jax.experimental.pallas import tpu as pltpu
from jax.sharding import PartitionSpec as P


def from_behind(value, axis, steps):
    count = lax.axis_size(axis)
    first, last = (max(0, -steps), min(count, count - steps))
    return lax.ppermute(value, axis, [(source, source + steps) for source in range(first, last)])


LANES = 128


def summary_kernel(decay_ref, product_ref, out_ref):
    poles, groups, lanes = out_ref.shape
    decay = jnp.broadcast_to(jnp.exp(-decay_ref[...])[:, None, :], (poles, groups, lanes))

    def step(t, state):
        return decay * state + product_ref[t][None]

    out_ref[...] = lax.fori_loop(0, product_ref.shape[0], step, jnp.zeros(out_ref.shape, jnp.float32))


def filter_kernel(decay_ref, residues_ref, skip_ref, product_ref, query_ref, incoming_ref, out_ref):
    poles, groups, lanes = incoming_ref.shape
    decay = jnp.broadcast_to(jnp.exp(-decay_ref[...])[:, None, :], (poles, groups, lanes))
    residues = residues_ref[...][:, None, :]
    skip = skip_ref[...]

    def step(t, state):
        product = product_ref[t]
        state = decay * state + product[None]
        out_ref[t] = query_ref[t] * (skip * product + jnp.sum(residues * state, axis=0))
        return state

    lax.fori_loop(0, product_ref.shape[0], step, incoming_ref[...])


def shards(tokens, norm_gain, w_in, taps, decay_rate, residues, skip_gain, w_out):
    values = tokens.astype(jnp.float32)
    inverse_rms = lax.rsqrt(jnp.mean(values * values, axis=-1, keepdims=True) + 1e-06)
    normed = (values * inverse_rms * norm_gain).astype(jnp.bfloat16)
    model_width = w_in.shape[0]
    channels = w_in.shape[2]
    w_flat = w_in.reshape(model_width, 3 * channels)
    features = jnp.einsum(
        "gtd,de->gte",
        lax.all_gather(normed, "fsdp", axis=0, tiled=True),
        w_flat,
        preferred_element_type=jnp.float32,
    ).astype(jnp.bfloat16)
    groups = features.shape[0]
    length = features.shape[1]
    poles = decay_rate.shape[0]
    edge_rows = from_behind(features[:, length - 2 :], "ctx", 1)
    extended = jnp.concatenate([edge_rows, features], axis=1).transpose(1, 0, 2).astype(jnp.float32)
    tap_rows = taps.reshape(taps.shape[0], 3 * channels)
    filtered = tap_rows[0] * extended[2:] + tap_rows[1] * extended[1:-1] + tap_rows[2] * extended[:-2]
    query_part = filtered[:, :, :channels]
    product = filtered[:, :, channels : 2 * channels] * filtered[:, :, 2 * channels :]
    pole_spec = pl.BlockSpec((poles, LANES), lambda c: (0, c))
    state_spec = pl.BlockSpec((poles, groups, LANES), lambda c: (0, 0, c))
    rows_spec = pl.BlockSpec((length, groups, LANES), lambda c: (0, 0, c))
    summary = pl.pallas_call(
        summary_kernel,
        grid=(channels // LANES,),
        in_specs=[pole_spec, rows_spec],
        out_specs=state_spec,
        out_shape=jax.ShapeDtypeStruct((poles, groups, channels), jnp.float32),
    )(decay_rate, product)
    decay_all = jnp.exp(-decay_rate * length)[:, None, :]
    incoming = jnp.zeros_like(summary)
    for hop_step in range(lax.axis_size("ctx") - 1):
        incoming = from_behind(
            (decay_all * incoming + summary).astype(jnp.bfloat16), "ctx", 1
        ).astype(jnp.float32)
    gated = pl.pallas_call(
        filter_kernel,
        grid=(channels // LANES,),
        in_specs=[pole_spec, pole_spec, pl.BlockSpec((1, LANES), lambda c: (0, c)), rows_spec, rows_spec, state_spec],
        out_specs=rows_spec,
        out_shape=jax.ShapeDtypeStruct((length, groups, channels), jnp.float32),
    )(decay_rate, residues, skip_gain[None], product, query_part, incoming)
    gated = gated.astype(jnp.bfloat16).transpose(1, 0, 2).reshape(groups * length, channels)
    summed = lax.psum_scatter(
        jnp.dot(gated, w_out, preferred_element_type=jnp.float32).astype(jnp.bfloat16),
        "fsdp",
        scatter_dimension=0,
        tiled=True,
    ).astype(jnp.float32)
    return (values[0] + summed).astype(jnp.bfloat16)[None]


CHUNKS = 4
COLUMNS = 256
STRIP = 16
UNROLL = 4
VMEM_BUDGET = 52 * 1024 * 1024
VMEM_LIMIT = 63 * 1024 * 1024


def fused_kernel(
    nz, nctx,
    tok, gain, w_in, taps, decay, residues, skip, w_out,
    out,
    w_v, wo_v, gat, part, rxx, rz, feat, prod, query, gated, gated_rows, edge_rx, st_tx, st_rx, inc, acc,
    w_sem, ag_send, ag_recv, x_send, x_recv, z_send, z_recv, edge_send, edge_recv, st_send, st_recv,
):
    T, D = tok.shape
    C = w_in.shape[2]
    J = C // LANES
    R = 2 * J
    NP = decay.shape[0]
    TC = T // CHUNKS
    f = lax.axis_index("fsdp")
    c = lax.axis_index("ctx")
    z = lax.div(f, 2)
    x = lax.rem(f, 2)
    partner = z * 2 + 1 - x
    has_left, has_right = z > 0, z < nz - 1

    w_copy = pltpu.make_async_copy(w_in, w_v, w_sem.at[0])
    wo_copy = pltpu.make_async_copy(w_out, wo_v, w_sem.at[1])
    w_copy.start()
    wo_copy.start()

    barrier = pltpu.get_barrier_semaphore()
    pl.semaphore_signal(barrier, inc=1, device_id={"fsdp": partner}, device_id_type=pl.DeviceIdType.MESH)

    @pl.when(has_left)
    def _():
        pl.semaphore_signal(barrier, inc=1, device_id={"fsdp": f - 2}, device_id_type=pl.DeviceIdType.MESH)

    @pl.when(has_right)
    def _():
        pl.semaphore_signal(barrier, inc=1, device_id={"fsdp": f + 2}, device_id_type=pl.DeviceIdType.MESH)

    for d in range(1, nctx):
        pl.semaphore_signal(
            barrier, inc=1, device_id={"ctx": lax.rem(c + d, nctx)}, device_id_type=pl.DeviceIdType.MESH
        )

    def rows(start, size):
        return pl.ds(pl.multiple_of(start, STRIP), size)

    @pl.loop(0, T // STRIP)
    def _(k):
        value = tok[rows(k * STRIP, STRIP), :].astype(jnp.float32)
        scale = lax.rsqrt(jnp.mean(value * value, axis=-1, keepdims=True) + 1e-06)
        gat[rows(f * T + k * STRIP, STRIP), :] = (value * scale * gain[...]).astype(jnp.bfloat16)

    pl.semaphore_wait(barrier, nctx + has_left.astype(jnp.int32) + has_right.astype(jnp.int32))

    def remote(src, dst, send, recv, device):
        return pltpu.make_async_remote_copy(
            src_ref=src, dst_ref=dst, send_sem=send, recv_sem=recv,
            device_id=device, device_id_type=pl.DeviceIdType.MESH,
        )

    X, UP, DOWN = 0, 1, 2

    def ag(block, ch, way):
        where = gat.at[rows(block * T + ch * TC, TC), :]
        target = {X: partner, UP: f + 2, DOWN: f - 2}[way]
        return remote(
            where, where, ag_send.at[way, lax.div(block, 2), ch], ag_recv.at[block, ch], {"fsdp": target}
        )

    def part_x(p, ch):
        return remote(
            part.at[rows((p * 2 + 1 - x) * T + ch * TC, TC), :],
            rxx.at[rows(p * T + ch * TC, TC), :],
            x_send.at[p, ch], x_recv.at[p, ch], {"fsdp": partner},
        )

    def part_z(p, ch, slot, target):
        return remote(
            part.at[rows((p * 2 + x) * T + ch * TC, TC), :],
            rz.at[rows(slot * T + ch * TC, TC), :],
            z_send.at[p, ch], z_recv.at[slot, ch], {"fsdp": target},
        )

    for ch in range(CHUNKS):
        ag(f, ch, X).start()

        @pl.when(has_right)
        def _():
            ag(f, ch, UP).start()

        @pl.when(has_left)
        def _():
            ag(f, ch, DOWN).start()

    def compute(p):
        @pl.loop(0, CHUNKS)
        def _(ch):
            ag(p * 2 + 1 - x, ch, X).wait_recv()

        for i in range(3):
            for n in range(C // COLUMNS):
                result = jnp.dot(
                    gat[rows(p * 2 * T, 2 * T), :],
                    w_v[i, :, n * COLUMNS : (n + 1) * COLUMNS],
                    preferred_element_type=jnp.float32,
                ).astype(jnp.bfloat16).astype(jnp.float32)
                for s in range(2):
                    for j in range(COLUMNS // LANES):
                        first = 2 * R + s * J + n * (COLUMNS // LANES) + j
                        feat[i, pl.ds(first, T, stride=R), :] = result[
                            s * T : (s + 1) * T, j * LANES : (j + 1) * LANES
                        ]

        edge = remote(
            feat.at[:, pl.ds(T * R, 2 * R), :], edge_rx.at[p], edge_send.at[p], edge_recv.at[p], {"ctx": c + 1}
        )

        @pl.when(c + 1 < nctx)
        def _():
            edge.start()

        @pl.when(c > 0)
        def _():
            edge.wait_recv()
            feat[:, 0 : 2 * R, :] = edge_rx[p]

        @pl.when(c == 0)
        def _():
            feat[:, 0 : 2 * R, :] = jnp.zeros((3, 2 * R, LANES), jnp.float32)

        def first_pass(block, state):
            decays = [jnp.exp(-decay[n]) for n in range(NP)]
            for k in range(UNROLL):
                base = (block * UNROLL + k) * R
                filtered = [
                    taps[0, i] * feat[i, pl.ds(pl.multiple_of(base + 2 * R, R), R), :]
                    + taps[1, i] * feat[i, pl.ds(pl.multiple_of(base + R, R), R), :]
                    + taps[2, i] * feat[i, pl.ds(pl.multiple_of(base, R), R), :]
                    for i in range(3)
                ]
                product = filtered[1] * filtered[2]
                prod[pl.ds(pl.multiple_of(base, R), R), :] = product
                query[pl.ds(pl.multiple_of(base, R), R), :] = filtered[0]
                state = tuple(decays[n] * state[n] + product for n in range(NP))
            return state

        zero = jnp.zeros((R, LANES), jnp.float32)
        state = lax.fori_loop(0, T // UNROLL, first_pass, (zero,) * NP)
        for n in range(NP):
            st_tx[p, n] = state[n]

        def state_copy(d):
            return remote(
                st_tx.at[p], st_rx.at[p, d - 1], st_send.at[p, d - 1], st_recv.at[p, d - 1], {"ctx": c + d}
            )

        for d in range(1, nctx):
            @pl.when(c + d < nctx)
            def _():
                state_copy(d).start()

        inc[...] = jnp.zeros(inc.shape, jnp.float32)
        for d in range(1, nctx):
            @pl.when(c >= d)
            def _():
                state_copy(d).wait_recv()
                inc[...] += jnp.exp(decay[...] * (-float(T * (d - 1)))) * st_rx[p, d - 1]

        def second_pass(block, state):
            decays = [jnp.exp(-decay[n]) for n in range(NP)]
            for k in range(UNROLL):
                here = pl.ds(pl.multiple_of((block * UNROLL + k) * R, R), R)
                product = prod[here, :]
                state = tuple(decays[n] * state[n] + product for n in range(NP))
                sums = [skip[...] * product] + [residues[n] * state[n] for n in range(NP)]
                while len(sums) > 1:
                    sums = [sum(sums[k : k + 2]) for k in range(0, len(sums), 2)]
                gated[here, :] = query[here, :] * sums[0]
            return state

        lax.fori_loop(0, T // UNROLL, second_pass, tuple(inc[n] for n in range(NP)))
        for s in range(2):
            for j in range(J):
                gated_rows[s * T : (s + 1) * T, j * LANES : (j + 1) * LANES] = gated[
                    pl.ds(s * J + j, T, stride=R), :
                ].astype(jnp.bfloat16)

        @pl.loop(0, D // COLUMNS)
        def _(n):
            where = pl.ds(pl.multiple_of(n * COLUMNS, COLUMNS), COLUMNS)
            part[rows(p * 2 * T, 2 * T), where] = jnp.dot(
                gated_rows[...], wo_v[:, where], preferred_element_type=jnp.float32
            ).astype(jnp.bfloat16)

        @pl.loop(0, CHUNKS)
        def _(ch):
            part_x(p, ch).start()

        @pl.when(c + 1 < nctx)
        def _():
            edge.wait_send()

        for d in range(1, nctx):
            @pl.when(c + d < nctx)
            def _():
                state_copy(d).wait_send()

    w_copy.wait()
    wo_copy.wait()

    def main_step(h, carry):
        @pl.when(h < nz)
        def _():
            @pl.loop(0, CHUNKS)
            def _(ch):
                @pl.when(z - h >= 0)
                def _():
                    block = (z - h) * 2 + x
                    ag(block, ch, UP).wait_recv()

                    @pl.when(has_right)
                    def _():
                        ag(block, ch, UP).start()

                    ag(block, ch, X).start()

                @pl.when(z + h < nz)
                def _():
                    block = (z + h) * 2 + x
                    ag(block, ch, DOWN).wait_recv()

                    @pl.when(has_left)
                    def _():
                        ag(block, ch, DOWN).start()

                    ag(block, ch, X).start()

        def side_step(side, carry):
            p = z + (h - 1) * (2 * side - 1)

            @pl.when((p >= 0) & (p < nz) & ((h > 1) | (side == 0)))
            def _():
                compute(p)

            return carry

        return lax.fori_loop(0, 2, side_step, carry)

    lax.fori_loop(1, nz + 1, main_step, 0)

    def load(ref, start, k):
        return ref[rows(start + k * STRIP, STRIP), :].astype(jnp.float32)

    def combine(p, ch, more):
        start = (p * 2 + x) * T + ch * TC
        other = p * T + ch * TC
        part_x(p, ch).wait_recv()

        @pl.when(more)
        def _():
            part_z(p, ch, p, partner).wait_recv()

            @pl.loop(0, TC // STRIP)
            def _(k):
                total = load(part, start, k) + load(rxx, other, k) + load(rz, other, k)
                part[rows(start + k * STRIP, STRIP), :] = total.astype(jnp.bfloat16)

        @pl.when(jnp.logical_not(more))
        def _():
            @pl.loop(0, TC // STRIP)
            def _(k):
                total = load(part, start, k) + load(rxx, other, k)
                part[rows(start + k * STRIP, STRIP), :] = total.astype(jnp.bfloat16)

    def reduce_step(i, carry):
        down = nz - 1 - i

        @pl.loop(0, CHUNKS)
        def _(ch):
            @pl.when(i > z)
            def _():
                combine(i, ch, has_left)
                part_z(i, ch, i, f + 2).start()

            @pl.when(down < z)
            def _():
                combine(down, ch, has_right)
                part_z(down, ch, jnp.where(down == z - 1, nz, down), f - 2).start()

        return carry

    lax.fori_loop(1, nz, reduce_step, 0)

    @pl.loop(0, CHUNKS)
    def _(ch):
        start = ch * TC
        part_x(z, ch).wait_recv()

        @pl.loop(0, TC // STRIP)
        def _(k):
            acc[rows(k * STRIP, STRIP), :] = (
                load(tok, start, k) + load(part, f * T + start, k) + load(rxx, z * T + start, k)
            )

        for more, slot in ((has_left, z), (has_right, nz)):
            @pl.when(more)
            def _():
                part_z(z, ch, slot, partner).wait_recv()

                @pl.loop(0, TC // STRIP)
                def _(k):
                    acc[rows(k * STRIP, STRIP), :] += load(rz, slot * T + start, k)

        @pl.loop(0, TC // STRIP)
        def _(k):
            out[rows(start + k * STRIP, STRIP), :] = acc[rows(k * STRIP, STRIP), :].astype(jnp.bfloat16)

    @pl.loop(0, nz)
    def _(p):
        @pl.loop(0, CHUNKS)
        def _(ch):
            ag(p * 2 + x, ch, X).wait_send()
            part_x(p, ch).wait_send()

            @pl.when((p <= z) & has_right)
            def _():
                ag(p * 2 + x, ch, UP).wait_send()

            @pl.when((p >= z) & has_left)
            def _():
                ag(p * 2 + x, ch, DOWN).wait_send()

            @pl.when(p != z)
            def _():
                part_z(p, ch, p, partner).wait_send()


def scratch_of(nz, nctx, T, D, C, NP):
    R = 2 * C // LANES
    f32, bf16 = jnp.float32, jnp.bfloat16
    arrays = [
        ((3, D, C), bf16),
        ((C, D), bf16),
        ((nz * 2 * T, D), bf16),
        ((nz * 2 * T, D), bf16),
        ((nz * T, D), bf16),
        (((nz + 1) * T, D), bf16),
        ((3, (T + 2) * R, LANES), f32),
        ((T * R, LANES), f32),
        ((T * R, LANES), f32),
        ((T * R, LANES), f32),
        ((2 * T, C), bf16),
        ((nz, 3, 2 * R, LANES), f32),
        ((nz, NP, R, LANES), f32),
        ((nz, nctx - 1, NP, R, LANES), f32),
        ((NP, R, LANES), f32),
        ((T // CHUNKS, D), f32),
    ]
    size = sum(functools.reduce(lambda a, b: a * b, shape) * jnp.dtype(kind).itemsize for shape, kind in arrays)
    return arrays, size


def fused_shards(nz, nctx, tokens, norm_gain, w_in, taps, decay_rate, residues, skip_gain, w_out):
    T, D = tokens.shape[1:]
    C = w_in.shape[2]
    NP = decay_rate.shape[0]

    def twice(value):
        value = value.reshape(value.shape[:-1] + (C // LANES, LANES))
        return jnp.concatenate([value, value], axis=-2)

    arrays, _ = scratch_of(nz, nctx, T, D, C, NP)
    dma = pltpu.SemaphoreType.DMA
    vmem, anywhere = pl.BlockSpec(memory_space=pltpu.VMEM), pl.BlockSpec(memory_space=pl.ANY)
    return pl.pallas_call(
        functools.partial(fused_kernel, nz, nctx),
        out_shape=jax.ShapeDtypeStruct((T, D), jnp.bfloat16),
        in_specs=[vmem, vmem, anywhere, vmem, vmem, vmem, vmem, anywhere],
        out_specs=vmem,
        scratch_shapes=[pltpu.VMEM(shape, kind) for shape, kind in arrays]
        + [
            dma((2,)),
            dma((3, nz, CHUNKS)),
            dma((2 * nz, CHUNKS)),
            dma((nz, CHUNKS)),
            dma((nz, CHUNKS)),
            dma((nz, CHUNKS)),
            dma((nz + 1, CHUNKS)),
            dma((nz,)),
            dma((nz,)),
            dma((nz, nctx - 1)),
            dma((nz, nctx - 1)),
        ],
        compiler_params=pltpu.CompilerParams(
            collective_id=0, has_side_effects=True, vmem_limit_bytes=VMEM_LIMIT
        ),
    )(
        tokens[0], norm_gain[None], w_in.transpose(1, 0, 2), twice(taps), twice(decay_rate),
        twice(residues), twice(skip_gain), w_out,
    )[None]


def solution(mesh):
    in_specs = (
        P("fsdp", "ctx", None),
        P(),
        P(None, None, "fsdp"),
        P(None, None, "fsdp"),
        P(None, "fsdp"),
        P(None, "fsdp"),
        P("fsdp"),
        P("fsdp", None),
    )
    out_specs = P("fsdp", "ctx", None)
    count, nctx = mesh.shape["fsdp"], mesh.shape["ctx"]

    def whole(tokens, norm_gain, w_in, *rest):
        D, channels = w_in.shape[0], w_in.shape[2] // count
        length, poles = tokens.shape[1] // nctx, rest[1].shape[0]
        _, size = scratch_of(count // 2, nctx, length, D, channels, poles)
        fits = size <= VMEM_BUDGET and count % 2 == 0 and tokens.shape[0] == count
        fits = fits and channels % (4 * LANES) == 0 and length % (CHUNKS * STRIP) == 0
        chosen = functools.partial(fused_shards, count // 2, nctx) if fits else shards
        return sharded(chosen)(tokens, norm_gain, w_in, *rest)

    def sharded(body):
        return jax.shard_map(body, mesh=mesh, in_specs=in_specs, out_specs=out_specs, check_vma=False)

    return whole
```

```python
import functools

import jax
import jax.numpy as jnp
from jax import lax
from jax.experimental import pallas as pl
from jax.experimental.pallas import tpu as pltpu
from jax.sharding import PartitionSpec as P


def from_behind(value, axis, steps):
    count = lax.axis_size(axis)
    first, last = (max(0, -steps), min(count, count - steps))
    return lax.ppermute(value, axis, [(source, source + steps) for source in range(first, last)])


LANES = 128


def summary_kernel(decay_ref, product_ref, out_ref):
    poles, groups, lanes = out_ref.shape
    decay = jnp.broadcast_to(jnp.exp(-decay_ref[...])[:, None, :], (poles, groups, lanes))

    def step(t, state):
        return decay * state + product_ref[t][None]

    out_ref[...] = lax.fori_loop(0, product_ref.shape[0], step, jnp.zeros(out_ref.shape, jnp.float32))


def filter_kernel(decay_ref, residues_ref, skip_ref, product_ref, query_ref, incoming_ref, out_ref):
    poles, groups, lanes = incoming_ref.shape
    decay = jnp.broadcast_to(jnp.exp(-decay_ref[...])[:, None, :], (poles, groups, lanes))
    residues = residues_ref[...][:, None, :]
    skip = skip_ref[...]

    def step(t, state):
        product = product_ref[t]
        state = decay * state + product[None]
        out_ref[t] = query_ref[t] * (skip * product + jnp.sum(residues * state, axis=0))
        return state

    lax.fori_loop(0, product_ref.shape[0], step, incoming_ref[...])


def shards(tokens, norm_gain, w_in, taps, decay_rate, residues, skip_gain, w_out):
    values = tokens.astype(jnp.float32)
    inverse_rms = lax.rsqrt(jnp.mean(values * values, axis=-1, keepdims=True) + 1e-06)
    normed = (values * inverse_rms * norm_gain).astype(jnp.bfloat16)
    model_width = w_in.shape[0]
    channels = w_in.shape[2]
    w_flat = w_in.reshape(model_width, 3 * channels)
    features = jnp.einsum(
        "gtd,de->gte",
        lax.all_gather(normed, "fsdp", axis=0, tiled=True),
        w_flat,
        preferred_element_type=jnp.float32,
    ).astype(jnp.bfloat16)
    groups = features.shape[0]
    length = features.shape[1]
    poles = decay_rate.shape[0]
    edge_rows = from_behind(features[:, length - 2 :], "ctx", 1)
    extended = jnp.concatenate([edge_rows, features], axis=1).transpose(1, 0, 2).astype(jnp.float32)
    tap_rows = taps.reshape(taps.shape[0], 3 * channels)
    filtered = tap_rows[0] * extended[2:] + tap_rows[1] * extended[1:-1] + tap_rows[2] * extended[:-2]
    query_part = filtered[:, :, :channels]
    product = filtered[:, :, channels : 2 * channels] * filtered[:, :, 2 * channels :]
    pole_spec = pl.BlockSpec((poles, LANES), lambda c: (0, c))
    state_spec = pl.BlockSpec((poles, groups, LANES), lambda c: (0, 0, c))
    rows_spec = pl.BlockSpec((length, groups, LANES), lambda c: (0, 0, c))
    summary = pl.pallas_call(
        summary_kernel,
        grid=(channels // LANES,),
        in_specs=[pole_spec, rows_spec],
        out_specs=state_spec,
        out_shape=jax.ShapeDtypeStruct((poles, groups, channels), jnp.float32),
    )(decay_rate, product)
    decay_all = jnp.exp(-decay_rate * length)[:, None, :]
    incoming = jnp.zeros_like(summary)
    for hop_step in range(lax.axis_size("ctx") - 1):
        incoming = from_behind(
            (decay_all * incoming + summary).astype(jnp.bfloat16), "ctx", 1
        ).astype(jnp.float32)
    gated = pl.pallas_call(
        filter_kernel,
        grid=(channels // LANES,),
        in_specs=[pole_spec, pole_spec, pl.BlockSpec((1, LANES), lambda c: (0, c)), rows_spec, rows_spec, state_spec],
        out_specs=rows_spec,
        out_shape=jax.ShapeDtypeStruct((length, groups, channels), jnp.float32),
    )(decay_rate, residues, skip_gain[None], product, query_part, incoming)
    gated = gated.astype(jnp.bfloat16).transpose(1, 0, 2).reshape(groups * length, channels)
    summed = lax.psum_scatter(
        jnp.dot(gated, w_out, preferred_element_type=jnp.float32).astype(jnp.bfloat16),
        "fsdp",
        scatter_dimension=0,
        tiled=True,
    ).astype(jnp.float32)
    return (values[0] + summed).astype(jnp.bfloat16)[None]


CHUNKS = 4
COLUMNS = 256
STRIP = 16
UNROLL = 4
VMEM_BUDGET = 52 * 1024 * 1024
VMEM_LIMIT = 63 * 1024 * 1024


def fused_kernel(
    nz, nctx,
    tok, gain, w_in, taps_in, decay_in, residues_in, skip_in, w_out,
    out,
    w_v, wo_v, gat, part, rxx, rz, feat, prod, query, gated, gated_rows, edge_rx, st_tx, st_rx, inc, acc, rzo,
    taps, decay, residues, skip,
    w_sem, ag_send, ag_recv, x_send, x_recv, z_send, z_recv, o_send, o_recv, edge_send, edge_recv, st_send, st_recv,
):
    T, D = tok.shape
    C = w_in.shape[2]
    J = C // LANES
    R = 2 * J
    NP = decay_in.shape[0]
    TC = T // CHUNKS
    f = lax.axis_index("fsdp")
    c = lax.axis_index("ctx")
    z = lax.div(f, 2)
    x = lax.rem(f, 2)
    partner = z * 2 + 1 - x
    has_left, has_right = z > 0, z < nz - 1

    w_copy = pltpu.make_async_copy(w_in, w_v, w_sem.at[0])
    wo_copy = pltpu.make_async_copy(w_out, wo_v, w_sem.at[1])
    w_copy.start()
    wo_copy.start()

    barrier = pltpu.get_barrier_semaphore()
    pl.semaphore_signal(barrier, inc=1, device_id={"fsdp": partner}, device_id_type=pl.DeviceIdType.MESH)

    @pl.when(has_left)
    def _():
        pl.semaphore_signal(barrier, inc=1, device_id={"fsdp": f - 2}, device_id_type=pl.DeviceIdType.MESH)

    @pl.when(has_right)
    def _():
        pl.semaphore_signal(barrier, inc=1, device_id={"fsdp": f + 2}, device_id_type=pl.DeviceIdType.MESH)

    for d in range(1, nctx):
        pl.semaphore_signal(
            barrier, inc=1, device_id={"ctx": lax.rem(c + d, nctx)}, device_id_type=pl.DeviceIdType.MESH
        )

    def rows(start, size):
        return pl.ds(pl.multiple_of(start, STRIP), size)

    def remote(src, dst, send, recv, device):
        return pltpu.make_async_remote_copy(
            src_ref=src, dst_ref=dst, send_sem=send, recv_sem=recv,
            device_id=device, device_id_type=pl.DeviceIdType.MESH,
        )

    X, UP, DOWN = 0, 1, 2

    def ag(block, ch, way):
        where = gat.at[rows(block * T + ch * TC, TC), :]
        target = {X: partner, UP: f + 2, DOWN: f - 2}[way]
        return remote(
            where, where, ag_send.at[way, block, ch], ag_recv.at[block, ch], {"fsdp": target}
        )

    def part_x(p, ch):
        return remote(
            part.at[rows((p * 2 + 1 - x) * T + ch * TC, TC), :],
            rxx.at[rows(p * T + ch * TC, TC), :],
            x_send.at[p, ch], x_recv.at[p, ch], {"fsdp": partner},
        )

    def part_z(p, ch, slot, target):
        return remote(
            part.at[rows((p * 2 + x) * T + ch * TC, TC), :],
            rz.at[rows(slot * T + ch * TC, TC), :],
            z_send.at[p, ch], z_recv.at[slot, ch], {"fsdp": target},
        )

    for ch in range(CHUNKS):
        @pl.loop(ch * (TC // STRIP), (ch + 1) * (TC // STRIP))
        def _(k):
            value = tok[rows(k * STRIP, STRIP), :].astype(jnp.float32)
            scale = lax.rsqrt(jnp.mean(value * value, axis=-1, keepdims=True) + 1e-06)
            gat[rows(f * T + k * STRIP, STRIP), :] = (value * scale * gain[...]).astype(jnp.bfloat16)

        if ch == 0:
            pl.semaphore_wait(barrier, nctx + has_left.astype(jnp.int32) + has_right.astype(jnp.int32))
        ag(f, ch, X).start()

        @pl.when(has_right)
        def _():
            ag(f, ch, UP).start()

        @pl.when(has_left)
        def _():
            ag(f, ch, DOWN).start()

    for s in range(2):
        for j in range(J):
            row, lanes = s * J + j, slice(j * LANES, (j + 1) * LANES)
            for n in range(NP):
                decay[n, row : row + 1, :] = decay_in[n : n + 1, lanes]
                residues[n, row : row + 1, :] = residues_in[n : n + 1, lanes]
            for k in range(3):
                for i in range(3):
                    taps[k, i, row : row + 1, :] = taps_in[k, i : i + 1, lanes]
            skip[row : row + 1, :] = skip_in[0:1, lanes]

    ag(partner, 0, X).wait_recv()

    @pl.when(has_right)
    def _():
        ag(partner, 0, UP).start()

    @pl.when(has_left)
    def _():
        ag(partner, 0, DOWN).start()

    def compute(p):
        @pl.loop(1, CHUNKS)
        def _(ch):
            ag(p * 2 + 1 - x, ch, X).wait_recv()

        for i in range(3):
            for n in range(C // COLUMNS):
                result = jnp.dot(
                    gat[rows(p * 2 * T, 2 * T), :],
                    w_v[i, :, n * COLUMNS : (n + 1) * COLUMNS],
                    preferred_element_type=jnp.float32,
                ).astype(jnp.bfloat16).astype(jnp.float32)
                for s in range(2):
                    for j in range(COLUMNS // LANES):
                        first = 2 * R + s * J + n * (COLUMNS // LANES) + j
                        feat[i, pl.ds(first, T, stride=R), :] = result[
                            s * T : (s + 1) * T, j * LANES : (j + 1) * LANES
                        ]

        edge = remote(
            feat.at[:, pl.ds(T * R, 2 * R), :], edge_rx.at[p], edge_send.at[p], edge_recv.at[p], {"ctx": c + 1}
        )

        @pl.when(c + 1 < nctx)
        def _():
            edge.start()

        @pl.when(c > 0)
        def _():
            edge.wait_recv()
            feat[:, 0 : 2 * R, :] = edge_rx[p]

        @pl.when(c == 0)
        def _():
            feat[:, 0 : 2 * R, :] = jnp.zeros((3, 2 * R, LANES), jnp.float32)

        def first_pass(block, state):
            decays = [jnp.exp(-decay[n]) for n in range(NP)]
            for k in range(UNROLL):
                base = (block * UNROLL + k) * R
                filtered = [
                    taps[0, i] * feat[i, pl.ds(pl.multiple_of(base + 2 * R, R), R), :]
                    + taps[1, i] * feat[i, pl.ds(pl.multiple_of(base + R, R), R), :]
                    + taps[2, i] * feat[i, pl.ds(pl.multiple_of(base, R), R), :]
                    for i in range(3)
                ]
                product = filtered[1] * filtered[2]
                prod[pl.ds(pl.multiple_of(base, R), R), :] = product
                query[pl.ds(pl.multiple_of(base, R), R), :] = filtered[0]
                state = tuple(decays[n] * state[n] + product for n in range(NP))
            return state

        zero = jnp.zeros((R, LANES), jnp.float32)
        state = lax.fori_loop(0, T // UNROLL, first_pass, (zero,) * NP)
        for n in range(NP):
            st_tx[p, n] = state[n]

        def state_copy(d):
            return remote(
                st_tx.at[p], st_rx.at[p, d - 1], st_send.at[p, d - 1], st_recv.at[p, d - 1], {"ctx": c + d}
            )

        for d in range(1, nctx):
            @pl.when(c + d < nctx)
            def _():
                state_copy(d).start()

        inc[...] = jnp.zeros(inc.shape, jnp.float32)
        for d in range(1, nctx):
            @pl.when(c >= d)
            def _():
                state_copy(d).wait_recv()
                inc[...] += jnp.exp(decay[...] * (-float(T * (d - 1)))) * st_rx[p, d - 1]

        def second_pass(block, state):
            decays = [jnp.exp(-decay[n]) for n in range(NP)]
            for k in range(UNROLL):
                here = pl.ds(pl.multiple_of((block * UNROLL + k) * R, R), R)
                product = prod[here, :]
                state = tuple(decays[n] * state[n] + product for n in range(NP))
                sums = [skip[...] * product] + [residues[n] * state[n] for n in range(NP)]
                while len(sums) > 1:
                    sums = [sum(sums[k : k + 2]) for k in range(0, len(sums), 2)]
                gated[here, :] = query[here, :] * sums[0]
            return state

        lax.fori_loop(0, T // UNROLL, second_pass, tuple(inc[n] for n in range(NP)))
        for s in range(2):
            for j in range(J):
                gated_rows[s * T : (s + 1) * T, j * LANES : (j + 1) * LANES] = gated[
                    pl.ds(s * J + j, T, stride=R), :
                ].astype(jnp.bfloat16)

        @pl.loop(0, D // COLUMNS)
        def _(n):
            where = pl.ds(pl.multiple_of(n * COLUMNS, COLUMNS), COLUMNS)
            part[rows(p * 2 * T, 2 * T), where] = jnp.dot(
                gated_rows[...], wo_v[:, where], preferred_element_type=jnp.float32
            ).astype(jnp.bfloat16)

        @pl.loop(1, CHUNKS)
        def _(ch):
            part_x(p, ch).start()

        @pl.when(c + 1 < nctx)
        def _():
            edge.wait_send()

        for d in range(1, nctx):
            @pl.when(c + d < nctx)
            def _():
                state_copy(d).wait_send()

    w_copy.wait()
    wo_copy.wait()

    def main_step(h, carry):
        @pl.when(h < nz)
        def _():
            def relay(block, ch, way):
                ag(block, ch, way).wait_recv()

                @pl.when(has_right if way == UP else has_left)
                def _():
                    ag(block, ch, way).start()

            for column in range(2):
                @pl.when(z - h >= 0)
                def _():
                    relay((z - h) * 2 + column, 0, UP)

                @pl.when(z + h < nz)
                def _():
                    relay((z + h) * 2 + column, 0, DOWN)

            @pl.loop(1, CHUNKS)
            def _(ch):
                @pl.when(z - h >= 0)
                def _():
                    block = (z - h) * 2 + x
                    relay(block, ch, UP)
                    ag(block, ch, X).start()

                @pl.when(z + h < nz)
                def _():
                    block = (z + h) * 2 + x
                    relay(block, ch, DOWN)
                    ag(block, ch, X).start()

        def side_step(side, carry):
            p = z + (h - 1) * (2 * side - 1)

            @pl.when((p >= 0) & (p < nz) & ((h > 1) | (side == 0)))
            def _():
                compute(p)

            return carry

        lax.fori_loop(0, 2, side_step, 0)

        @pl.when(h > 2)
        def _():
            reduce_step(h - 2)

        return carry

    def load(ref, start, k):
        return ref[rows(start + k * STRIP, STRIP), :].astype(jnp.float32)

    def combine(p, ch, more):
        start = (p * 2 + x) * T + ch * TC
        other = p * T + ch * TC
        part_x(p, ch).wait_recv()

        @pl.when(more)
        def _():
            part_z(p, ch, p, partner).wait_recv()

            @pl.loop(0, TC // STRIP)
            def _(k):
                total = load(part, start, k) + load(rxx, other, k) + load(rz, other, k)
                part[rows(start + k * STRIP, STRIP), :] = total.astype(jnp.bfloat16)

        @pl.when(jnp.logical_not(more))
        def _():
            @pl.loop(0, TC // STRIP)
            def _(k):
                total = load(part, start, k) + load(rxx, other, k)
                part[rows(start + k * STRIP, STRIP), :] = total.astype(jnp.bfloat16)

    def other_z(p, slot, target):
        return remote(
            part.at[rows((p * 2 + 1 - x) * T, TC), :],
            rzo.at[rows(slot * TC, TC), :],
            o_send.at[p], o_recv.at[slot], {"fsdp": target},
        )

    def add_in(start, ref, begin):
        @pl.loop(0, TC // STRIP)
        def _(k):
            total = load(part, start, k) + load(ref, begin, k)
            part[rows(start + k * STRIP, STRIP), :] = total.astype(jnp.bfloat16)

    def first_chunk(p, more, slot, target):
        @pl.when(more)
        def _():
            part_z(p, 0, p, partner).wait_recv()
            add_in((p * 2 + x) * T, rz, p * T)

        part_z(p, 0, slot, target).start()

        @pl.when(more)
        def _():
            other_z(p, p, partner).wait_recv()
            add_in((p * 2 + 1 - x) * T, rzo, p * TC)

        other_z(p, slot, target).start()

    def reduce_step(i):
        down = nz - 1 - i
        down_slot = jnp.where(down == z - 1, nz, down)

        @pl.when(i > z)
        def _():
            first_chunk(i, has_left, i, f + 2)

        @pl.when(down < z)
        def _():
            first_chunk(down, has_right, down_slot, f - 2)

        @pl.loop(1, CHUNKS)
        def _(ch):
            @pl.when(i > z)
            def _():
                combine(i, ch, has_left)
                part_z(i, ch, i, f + 2).start()

            @pl.when(down < z)
            def _():
                combine(down, ch, has_right)
                part_z(down, ch, down_slot, f - 2).start()

    lax.fori_loop(1, nz + 1, main_step, 0)
    reduce_step(nz - 1)

    for more, slot in ((has_left, z), (has_right, nz)):
        @pl.when(more)
        def _():
            other_z(z, slot, partner).wait_recv()
            add_in(partner * T, rzo, slot * TC)

    part_x(z, 0).start()

    @pl.loop(0, CHUNKS)
    def _(turn):
        ch = lax.rem(turn + 1, CHUNKS)
        start = ch * TC
        part_x(z, ch).wait_recv()

        @pl.loop(0, TC // STRIP)
        def _(k):
            acc[rows(k * STRIP, STRIP), :] = (
                load(tok, start, k) + load(part, f * T + start, k) + load(rxx, z * T + start, k)
            )

        for more, slot in ((has_left, z), (has_right, nz)):
            @pl.when(more)
            def _():
                part_z(z, ch, slot, partner).wait_recv()

                @pl.loop(0, TC // STRIP)
                def _(k):
                    acc[rows(k * STRIP, STRIP), :] += load(rz, slot * T + start, k)

        @pl.loop(0, TC // STRIP)
        def _(k):
            out[rows(start + k * STRIP, STRIP), :] = acc[rows(k * STRIP, STRIP), :].astype(jnp.bfloat16)

    @pl.loop(0, nz)
    def _(p):
        @pl.loop(0, CHUNKS)
        def _(ch):
            @pl.when((ch > 0) | (p == z))
            def _():
                ag(p * 2 + x, ch, X).wait_send()
                part_x(p, ch).wait_send()

            @pl.when((p <= z) & has_right)
            def _():
                ag(p * 2 + x, ch, UP).wait_send()

            @pl.when((p >= z) & has_left)
            def _():
                ag(p * 2 + x, ch, DOWN).wait_send()

            @pl.when(p != z)
            def _():
                part_z(p, ch, p, partner).wait_send()

        @pl.when((p <= z) & has_right)
        def _():
            ag(p * 2 + 1 - x, 0, UP).wait_send()

        @pl.when((p >= z) & has_left)
        def _():
            ag(p * 2 + 1 - x, 0, DOWN).wait_send()

        @pl.when(p != z)
        def _():
            other_z(p, p, partner).wait_send()


def scratch_of(nz, nctx, T, D, C, NP):
    R = 2 * C // LANES
    f32, bf16 = jnp.float32, jnp.bfloat16
    arrays = [
        ((3, D, C), bf16),
        ((C, D), bf16),
        ((nz * 2 * T, D), bf16),
        ((nz * 2 * T, D), bf16),
        ((nz * T, D), bf16),
        (((nz + 1) * T, D), bf16),
        ((3, (T + 2) * R, LANES), f32),
        ((T * R, LANES), f32),
        ((T * R, LANES), f32),
        ((T * R, LANES), f32),
        ((2 * T, C), bf16),
        ((nz, 3, 2 * R, LANES), f32),
        ((nz, NP, R, LANES), f32),
        ((nz, nctx - 1, NP, R, LANES), f32),
        ((NP, R, LANES), f32),
        ((T // CHUNKS, D), f32),
        (((nz + 1) * T // CHUNKS, D), bf16),
        ((3, 3, R, LANES), f32),
        ((NP, R, LANES), f32),
        ((NP, R, LANES), f32),
        ((R, LANES), f32),
    ]
    size = sum(functools.reduce(lambda a, b: a * b, shape) * jnp.dtype(kind).itemsize for shape, kind in arrays)
    return arrays, size


def fused_shards(nz, nctx, tokens, norm_gain, w_in, taps, decay_rate, residues, skip_gain, w_out):
    T, D = tokens.shape[1:]
    C = w_in.shape[2]
    NP = decay_rate.shape[0]

    arrays, _ = scratch_of(nz, nctx, T, D, C, NP)
    dma = pltpu.SemaphoreType.DMA
    vmem, anywhere = pl.BlockSpec(memory_space=pltpu.VMEM), pl.BlockSpec(memory_space=pl.ANY)
    return pl.pallas_call(
        functools.partial(fused_kernel, nz, nctx),
        out_shape=jax.ShapeDtypeStruct((T, D), jnp.bfloat16),
        in_specs=[vmem, vmem, anywhere, vmem, vmem, vmem, vmem, anywhere],
        out_specs=vmem,
        scratch_shapes=[pltpu.VMEM(shape, kind) for shape, kind in arrays]
        + [
            dma((2,)),
            dma((3, 2 * nz, CHUNKS)),
            dma((2 * nz, CHUNKS)),
            dma((nz, CHUNKS)),
            dma((nz, CHUNKS)),
            dma((nz, CHUNKS)),
            dma((nz + 1, CHUNKS)),
            dma((nz,)),
            dma((nz + 1,)),
            dma((nz,)),
            dma((nz,)),
            dma((nz, nctx - 1)),
            dma((nz, nctx - 1)),
        ],
        compiler_params=pltpu.CompilerParams(
            collective_id=0, has_side_effects=True, vmem_limit_bytes=VMEM_LIMIT
        ),
    )(
        tokens[0], norm_gain[None], w_in.transpose(1, 0, 2), taps, decay_rate, residues, skip_gain[None], w_out,
    )[None]


def solution(mesh):
    in_specs = (
        P("fsdp", "ctx", None),
        P(),
        P(None, None, "fsdp"),
        P(None, None, "fsdp"),
        P(None, "fsdp"),
        P(None, "fsdp"),
        P("fsdp"),
        P("fsdp", None),
    )
    out_specs = P("fsdp", "ctx", None)
    count, nctx = mesh.shape["fsdp"], mesh.shape["ctx"]

    def whole(tokens, norm_gain, w_in, *rest):
        D, channels = w_in.shape[0], w_in.shape[2] // count
        length, poles = tokens.shape[1] // nctx, rest[1].shape[0]
        _, size = scratch_of(count // 2, nctx, length, D, channels, poles)
        fits = size <= VMEM_BUDGET and count % 2 == 0 and tokens.shape[0] == count
        fits = fits and channels % (4 * LANES) == 0 and length % (CHUNKS * STRIP) == 0
        chosen = functools.partial(fused_shards, count // 2, nctx) if fits else shards
        return sharded(chosen)(tokens, norm_gain, w_in, *rest)

    def sharded(body):
        return jax.shard_map(body, mesh=mesh, in_specs=in_specs, out_specs=out_specs, check_vma=False)

    return whole
```

```python
import functools

import jax
import jax.numpy as jnp
from jax import lax
from jax.experimental import pallas as pl
from jax.experimental.pallas import tpu as pltpu
from jax.sharding import PartitionSpec as P


def from_behind(value, axis, steps):
    count = lax.axis_size(axis)
    first, last = (max(0, -steps), min(count, count - steps))
    return lax.ppermute(value, axis, [(source, source + steps) for source in range(first, last)])


LANES = 128


def summary_kernel(decay_ref, product_ref, out_ref):
    poles, groups, lanes = out_ref.shape
    decay = jnp.broadcast_to(jnp.exp(-decay_ref[...])[:, None, :], (poles, groups, lanes))

    def step(t, state):
        return decay * state + product_ref[t][None]

    out_ref[...] = lax.fori_loop(0, product_ref.shape[0], step, jnp.zeros(out_ref.shape, jnp.float32))


def filter_kernel(decay_ref, residues_ref, skip_ref, product_ref, query_ref, incoming_ref, out_ref):
    poles, groups, lanes = incoming_ref.shape
    decay = jnp.broadcast_to(jnp.exp(-decay_ref[...])[:, None, :], (poles, groups, lanes))
    residues = residues_ref[...][:, None, :]
    skip = skip_ref[...]

    def step(t, state):
        product = product_ref[t]
        state = decay * state + product[None]
        out_ref[t] = query_ref[t] * (skip * product + jnp.sum(residues * state, axis=0))
        return state

    lax.fori_loop(0, product_ref.shape[0], step, incoming_ref[...])


def shards(tokens, norm_gain, w_in, taps, decay_rate, residues, skip_gain, w_out):
    values = tokens.astype(jnp.float32)
    inverse_rms = lax.rsqrt(jnp.mean(values * values, axis=-1, keepdims=True) + 1e-06)
    normed = (values * inverse_rms * norm_gain).astype(jnp.bfloat16)
    model_width = w_in.shape[0]
    channels = w_in.shape[2]
    w_flat = w_in.reshape(model_width, 3 * channels)
    features = jnp.einsum(
        "gtd,de->gte",
        lax.all_gather(normed, "fsdp", axis=0, tiled=True),
        w_flat,
        preferred_element_type=jnp.float32,
    ).astype(jnp.bfloat16)
    groups = features.shape[0]
    length = features.shape[1]
    poles = decay_rate.shape[0]
    edge_rows = from_behind(features[:, length - 2 :], "ctx", 1)
    extended = jnp.concatenate([edge_rows, features], axis=1).transpose(1, 0, 2).astype(jnp.float32)
    tap_rows = taps.reshape(taps.shape[0], 3 * channels)
    filtered = tap_rows[0] * extended[2:] + tap_rows[1] * extended[1:-1] + tap_rows[2] * extended[:-2]
    query_part = filtered[:, :, :channels]
    product = filtered[:, :, channels : 2 * channels] * filtered[:, :, 2 * channels :]
    pole_spec = pl.BlockSpec((poles, LANES), lambda c: (0, c))
    state_spec = pl.BlockSpec((poles, groups, LANES), lambda c: (0, 0, c))
    rows_spec = pl.BlockSpec((length, groups, LANES), lambda c: (0, 0, c))
    summary = pl.pallas_call(
        summary_kernel,
        grid=(channels // LANES,),
        in_specs=[pole_spec, rows_spec],
        out_specs=state_spec,
        out_shape=jax.ShapeDtypeStruct((poles, groups, channels), jnp.float32),
    )(decay_rate, product)
    decay_all = jnp.exp(-decay_rate * length)[:, None, :]
    incoming = jnp.zeros_like(summary)
    for hop_step in range(lax.axis_size("ctx") - 1):
        incoming = from_behind(
            (decay_all * incoming + summary).astype(jnp.bfloat16), "ctx", 1
        ).astype(jnp.float32)
    gated = pl.pallas_call(
        filter_kernel,
        grid=(channels // LANES,),
        in_specs=[pole_spec, pole_spec, pl.BlockSpec((1, LANES), lambda c: (0, c)), rows_spec, rows_spec, state_spec],
        out_specs=rows_spec,
        out_shape=jax.ShapeDtypeStruct((length, groups, channels), jnp.float32),
    )(decay_rate, residues, skip_gain[None], product, query_part, incoming)
    gated = gated.astype(jnp.bfloat16).transpose(1, 0, 2).reshape(groups * length, channels)
    summed = lax.psum_scatter(
        jnp.dot(gated, w_out, preferred_element_type=jnp.float32).astype(jnp.bfloat16),
        "fsdp",
        scatter_dimension=0,
        tiled=True,
    ).astype(jnp.float32)
    return (values[0] + summed).astype(jnp.bfloat16)[None]


CHUNKS = 4
COLUMNS = 256
STRIP = 16
UNROLL = 4
VMEM_BUDGET = 52 * 1024 * 1024
VMEM_LIMIT = 63 * 1024 * 1024


def fused_kernel(
    nz, nctx,
    tok, gain, w_in, taps_in, decay_in, residues_in, skip_in, w_out,
    out,
    w_v, wo_v, gat, part, rxx, rz, feat, prod, query, gated, gated_rows, edge_rx, st_tx, st_rx, inc, acc, rzo,
    taps, decay, residues, skip, factor,
    w_sem, ag_send, ag_recv, x_send, x_recv, z_send, z_recv, o_send, o_recv, edge_send, edge_recv, st_send, st_recv,
):
    T, D = tok.shape
    C = w_in.shape[2]
    J = C // LANES
    R = 2 * J
    NP = decay_in.shape[0]
    TC = T // CHUNKS
    f = lax.axis_index("fsdp")
    c = lax.axis_index("ctx")
    z = lax.div(f, 2)
    x = lax.rem(f, 2)
    partner = z * 2 + 1 - x
    has_left, has_right = z > 0, z < nz - 1

    w_copy = pltpu.make_async_copy(w_in, w_v, w_sem.at[0])
    wo_copy = pltpu.make_async_copy(w_out, wo_v, w_sem.at[1])
    w_copy.start()
    wo_copy.start()

    barrier = pltpu.get_barrier_semaphore()
    pl.semaphore_signal(barrier, inc=1, device_id={"fsdp": partner}, device_id_type=pl.DeviceIdType.MESH)

    @pl.when(has_left)
    def _():
        pl.semaphore_signal(barrier, inc=1, device_id={"fsdp": f - 2}, device_id_type=pl.DeviceIdType.MESH)

    @pl.when(has_right)
    def _():
        pl.semaphore_signal(barrier, inc=1, device_id={"fsdp": f + 2}, device_id_type=pl.DeviceIdType.MESH)

    for d in range(1, nctx):
        pl.semaphore_signal(
            barrier, inc=1, device_id={"ctx": lax.rem(c + d, nctx)}, device_id_type=pl.DeviceIdType.MESH
        )

    def rows(start, size):
        return pl.ds(pl.multiple_of(start, STRIP), size)

    def remote(src, dst, send, recv, device):
        return pltpu.make_async_remote_copy(
            src_ref=src, dst_ref=dst, send_sem=send, recv_sem=recv,
            device_id=device, device_id_type=pl.DeviceIdType.MESH,
        )

    X, UP, DOWN = 0, 1, 2

    def ag(block, ch, way):
        where = gat.at[rows(block * T + ch * TC, TC), :]
        target = {X: partner, UP: f + 2, DOWN: f - 2}[way]
        return remote(
            where, where, ag_send.at[way, block, ch], ag_recv.at[block, ch], {"fsdp": target}
        )

    def part_x(p, ch):
        return remote(
            part.at[rows((p * 2 + 1 - x) * T + ch * TC, TC), :],
            rxx.at[rows(p * T + ch * TC, TC), :],
            x_send.at[p, ch], x_recv.at[p, ch], {"fsdp": partner},
        )

    def part_z(p, ch, slot, target):
        return remote(
            part.at[rows((p * 2 + x) * T + ch * TC, TC), :],
            rz.at[rows(slot * T + ch * TC, TC), :],
            z_send.at[p, ch], z_recv.at[slot, ch], {"fsdp": target},
        )

    for ch in range(CHUNKS):
        @pl.loop(ch * (TC // STRIP), (ch + 1) * (TC // STRIP))
        def _(k):
            value = tok[rows(k * STRIP, STRIP), :].astype(jnp.float32)
            scale = lax.rsqrt(jnp.mean(value * value, axis=-1, keepdims=True) + 1e-06)
            gat[rows(f * T + k * STRIP, STRIP), :] = (value * scale * gain[...]).astype(jnp.bfloat16)

        if ch == 0:
            pl.semaphore_wait(barrier, nctx + has_left.astype(jnp.int32) + has_right.astype(jnp.int32))
        ag(f, ch, X).start()

        @pl.when(has_right)
        def _():
            ag(f, ch, UP).start()

        @pl.when(has_left)
        def _():
            ag(f, ch, DOWN).start()

    for s in range(2):
        for j in range(J):
            row, lanes = s * J + j, slice(j * LANES, (j + 1) * LANES)
            for n in range(NP):
                decay[n, row : row + 1, :] = decay_in[n : n + 1, lanes]
                residues[n, row : row + 1, :] = residues_in[n : n + 1, lanes]
            for k in range(3):
                for i in range(3):
                    taps[k, i, row : row + 1, :] = taps_in[k, i : i + 1, lanes]
            skip[row : row + 1, :] = skip_in[0:1, lanes]
    factor[...] = jnp.exp(-decay[...])

    ag(partner, 0, X).wait_recv()

    @pl.when(has_right)
    def _():
        ag(partner, 0, UP).start()

    @pl.when(has_left)
    def _():
        ag(partner, 0, DOWN).start()

    def compute(p):
        @pl.loop(1, CHUNKS)
        def _(ch):
            ag(p * 2 + 1 - x, ch, X).wait_recv()

        for i in range(3):
            for n in range(C // COLUMNS):
                result = jnp.dot(
                    gat[rows(p * 2 * T, 2 * T), :],
                    w_v[i, :, n * COLUMNS : (n + 1) * COLUMNS],
                    preferred_element_type=jnp.float32,
                ).astype(jnp.bfloat16).astype(jnp.float32)
                for s in range(2):
                    for j in range(COLUMNS // LANES):
                        first = 2 * R + s * J + n * (COLUMNS // LANES) + j
                        feat[i, pl.ds(first, T, stride=R), :] = result[
                            s * T : (s + 1) * T, j * LANES : (j + 1) * LANES
                        ]

        edge = remote(
            feat.at[:, pl.ds(T * R, 2 * R), :], edge_rx.at[p], edge_send.at[p], edge_recv.at[p], {"ctx": c + 1}
        )

        @pl.when(c + 1 < nctx)
        def _():
            edge.start()

        def filter_row(base):
            filtered = [
                taps[0, i] * feat[i, pl.ds(pl.multiple_of(base + 2 * R, R), R), :]
                + taps[1, i] * feat[i, pl.ds(pl.multiple_of(base + R, R), R), :]
                + taps[2, i] * feat[i, pl.ds(pl.multiple_of(base, R), R), :]
                for i in range(3)
            ]
            product = filtered[1] * filtered[2]
            prod[pl.ds(pl.multiple_of(base, R), R), :] = product
            query[pl.ds(pl.multiple_of(base, R), R), :] = filtered[0]
            return product

        def first_pass(block, state):
            decays = [factor[n] for n in range(NP)]
            for k in range(UNROLL):
                base = (block * UNROLL + k) * R
                product = filter_row(base)
                state = tuple(decays[n] * state[n] + product for n in range(NP))
            return state

        state = (jnp.zeros((R, LANES), jnp.float32),) * NP
        for t in range(2, UNROLL):
            product = filter_row(t * R)
            state = tuple(factor[n] * state[n] + product for n in range(NP))
        state = lax.fori_loop(1, T // UNROLL, first_pass, state)
        for n in range(NP):
            st_tx[p, n] = state[n]

        @pl.when(c > 0)
        def _():
            edge.wait_recv()
            feat[:, 0 : 2 * R, :] = edge_rx[p]

        @pl.when(c == 0)
        def _():
            feat[:, 0 : 2 * R, :] = jnp.zeros((3, 2 * R, LANES), jnp.float32)

        early = [filter_row(t * R) for t in range(2)]
        for n in range(NP):
            st_tx[p, n] += (factor[n] * early[0] + early[1]) * jnp.exp(decay[n] * (-float(T - 2)))

        def state_copy(d):
            return remote(
                st_tx.at[p], st_rx.at[p, d - 1], st_send.at[p, d - 1], st_recv.at[p, d - 1], {"ctx": c + d}
            )

        for d in range(1, nctx):
            @pl.when(c + d < nctx)
            def _():
                state_copy(d).start()

        inc[...] = jnp.zeros(inc.shape, jnp.float32)
        for d in range(1, nctx):
            @pl.when(c >= d)
            def _():
                state_copy(d).wait_recv()
                inc[...] += jnp.exp(decay[...] * (-float(T * (d - 1)))) * st_rx[p, d - 1]

        def second_pass(block, state):
            decays = [factor[n] for n in range(NP)]
            for k in range(UNROLL):
                here = pl.ds(pl.multiple_of((block * UNROLL + k) * R, R), R)
                product = prod[here, :]
                state = tuple(decays[n] * state[n] + product for n in range(NP))
                sums = [skip[...] * product] + [residues[n] * state[n] for n in range(NP)]
                while len(sums) > 1:
                    sums = [sum(sums[k : k + 2]) for k in range(0, len(sums), 2)]
                gated[here, :] = query[here, :] * sums[0]
            return state

        lax.fori_loop(0, T // UNROLL, second_pass, tuple(inc[n] for n in range(NP)))
        for s in range(2):
            for j in range(J):
                gated_rows[s * T : (s + 1) * T, j * LANES : (j + 1) * LANES] = gated[
                    pl.ds(s * J + j, T, stride=R), :
                ].astype(jnp.bfloat16)

        @pl.loop(0, D // COLUMNS)
        def _(n):
            where = pl.ds(pl.multiple_of(n * COLUMNS, COLUMNS), COLUMNS)
            part[rows(p * 2 * T, 2 * T), where] = jnp.dot(
                gated_rows[...], wo_v[:, where], preferred_element_type=jnp.float32
            ).astype(jnp.bfloat16)

        @pl.loop(1, CHUNKS)
        def _(ch):
            part_x(p, ch).start()

        @pl.when(c + 1 < nctx)
        def _():
            edge.wait_send()

        for d in range(1, nctx):
            @pl.when(c + d < nctx)
            def _():
                state_copy(d).wait_send()

    w_copy.wait()
    wo_copy.wait()

    def main_step(h, carry):
        @pl.when(h < nz)
        def _():
            def relay(block, ch, way):
                ag(block, ch, way).wait_recv()

                @pl.when(has_right if way == UP else has_left)
                def _():
                    ag(block, ch, way).start()

            for column in range(2):
                @pl.when(z - h >= 0)
                def _():
                    relay((z - h) * 2 + column, 0, UP)

                @pl.when(z + h < nz)
                def _():
                    relay((z + h) * 2 + column, 0, DOWN)

            @pl.loop(1, CHUNKS)
            def _(ch):
                @pl.when(z - h >= 0)
                def _():
                    block = (z - h) * 2 + x
                    relay(block, ch, UP)
                    ag(block, ch, X).start()

                @pl.when(z + h < nz)
                def _():
                    block = (z + h) * 2 + x
                    relay(block, ch, DOWN)
                    ag(block, ch, X).start()

        def side_step(side, carry):
            p = z + (h - 1) * (2 * side - 1)

            @pl.when((p >= 0) & (p < nz) & ((h > 1) | (side == 0)))
            def _():
                compute(p)

            return carry

        lax.fori_loop(0, 2, side_step, 0)

        @pl.when(h > 2)
        def _():
            reduce_step(h - 2)

        return carry

    def load(ref, start, k):
        return ref[rows(start + k * STRIP, STRIP), :].astype(jnp.float32)

    def combine(p, ch, more):
        start = (p * 2 + x) * T + ch * TC
        other = p * T + ch * TC
        part_x(p, ch).wait_recv()

        @pl.when(more)
        def _():
            part_z(p, ch, p, partner).wait_recv()

            @pl.loop(0, TC // STRIP)
            def _(k):
                total = load(part, start, k) + load(rxx, other, k) + load(rz, other, k)
                part[rows(start + k * STRIP, STRIP), :] = total.astype(jnp.bfloat16)

        @pl.when(jnp.logical_not(more))
        def _():
            @pl.loop(0, TC // STRIP)
            def _(k):
                total = load(part, start, k) + load(rxx, other, k)
                part[rows(start + k * STRIP, STRIP), :] = total.astype(jnp.bfloat16)

    def other_z(p, slot, target):
        return remote(
            part.at[rows((p * 2 + 1 - x) * T, TC), :],
            rzo.at[rows(slot * TC, TC), :],
            o_send.at[p], o_recv.at[slot], {"fsdp": target},
        )

    def add_in(start, ref, begin):
        @pl.loop(0, TC // STRIP)
        def _(k):
            total = load(part, start, k) + load(ref, begin, k)
            part[rows(start + k * STRIP, STRIP), :] = total.astype(jnp.bfloat16)

    def first_chunk(p, more, slot, target):
        @pl.when(more)
        def _():
            part_z(p, 0, p, partner).wait_recv()
            add_in((p * 2 + x) * T, rz, p * T)

        part_z(p, 0, slot, target).start()

        @pl.when(more)
        def _():
            other_z(p, p, partner).wait_recv()
            add_in((p * 2 + 1 - x) * T, rzo, p * TC)

        other_z(p, slot, target).start()

    def send_sum(p, ch, more, slot, target):
        @pl.when(ch == 0)
        def _():
            first_chunk(p, more, slot, target)

        @pl.when(ch > 0)
        def _():
            combine(p, ch, more)
            part_z(p, ch, slot, target).start()

    up_late = (2 * z >= nz).astype(jnp.int32)

    def reduce_step(i):
        down = nz - 1 - i
        down_slot = jnp.where(down == z - 1, nz, down)

        @pl.loop(0, CHUNKS + 1)
        def _(turn):
            up_ch, down_ch = turn - up_late, turn - 1 + up_late

            @pl.when((i > z) & (up_ch >= 0) & (up_ch < CHUNKS))
            def _():
                send_sum(i, up_ch, has_left, i, f + 2)

            @pl.when((down < z) & (down_ch >= 0) & (down_ch < CHUNKS))
            def _():
                send_sum(down, down_ch, has_right, down_slot, f - 2)

    lax.fori_loop(1, nz + 1, main_step, 0)
    reduce_step(nz - 1)

    for more, slot in ((has_left, z), (has_right, nz)):
        @pl.when(more)
        def _():
            other_z(z, slot, partner).wait_recv()
            add_in(partner * T, rzo, slot * TC)

    part_x(z, 0).start()

    @pl.loop(0, CHUNKS)
    def _(turn):
        ch = lax.rem(turn + 1, CHUNKS)
        start = ch * TC
        part_x(z, ch).wait_recv()

        @pl.loop(0, TC // STRIP)
        def _(k):
            acc[rows(k * STRIP, STRIP), :] = (
                load(tok, start, k) + load(part, f * T + start, k) + load(rxx, z * T + start, k)
            )

        for more, slot in ((has_left, z), (has_right, nz)):
            @pl.when(more)
            def _():
                part_z(z, ch, slot, partner).wait_recv()

                @pl.loop(0, TC // STRIP)
                def _(k):
                    acc[rows(k * STRIP, STRIP), :] += load(rz, slot * T + start, k)

        @pl.loop(0, TC // STRIP)
        def _(k):
            out[rows(start + k * STRIP, STRIP), :] = acc[rows(k * STRIP, STRIP), :].astype(jnp.bfloat16)

    @pl.loop(0, nz)
    def _(p):
        @pl.loop(0, CHUNKS)
        def _(ch):
            @pl.when((ch > 0) | (p == z))
            def _():
                ag(p * 2 + x, ch, X).wait_send()
                part_x(p, ch).wait_send()

            @pl.when((p <= z) & has_right)
            def _():
                ag(p * 2 + x, ch, UP).wait_send()

            @pl.when((p >= z) & has_left)
            def _():
                ag(p * 2 + x, ch, DOWN).wait_send()

            @pl.when(p != z)
            def _():
                part_z(p, ch, p, partner).wait_send()

        @pl.when((p <= z) & has_right)
        def _():
            ag(p * 2 + 1 - x, 0, UP).wait_send()

        @pl.when((p >= z) & has_left)
        def _():
            ag(p * 2 + 1 - x, 0, DOWN).wait_send()

        @pl.when(p != z)
        def _():
            other_z(p, p, partner).wait_send()


def scratch_of(nz, nctx, T, D, C, NP):
    R = 2 * C // LANES
    f32, bf16 = jnp.float32, jnp.bfloat16
    arrays = [
        ((3, D, C), bf16),
        ((C, D), bf16),
        ((nz * 2 * T, D), bf16),
        ((nz * 2 * T, D), bf16),
        ((nz * T, D), bf16),
        (((nz + 1) * T, D), bf16),
        ((3, (T + 2) * R, LANES), f32),
        ((T * R, LANES), f32),
        ((T * R, LANES), f32),
        ((T * R, LANES), f32),
        ((2 * T, C), bf16),
        ((nz, 3, 2 * R, LANES), f32),
        ((nz, NP, R, LANES), f32),
        ((nz, nctx - 1, NP, R, LANES), f32),
        ((NP, R, LANES), f32),
        ((T // CHUNKS, D), f32),
        (((nz + 1) * T // CHUNKS, D), bf16),
        ((3, 3, R, LANES), f32),
        ((NP, R, LANES), f32),
        ((NP, R, LANES), f32),
        ((R, LANES), f32),
        ((NP, R, LANES), f32),
    ]
    size = sum(functools.reduce(lambda a, b: a * b, shape) * jnp.dtype(kind).itemsize for shape, kind in arrays)
    return arrays, size


def fused_shards(nz, nctx, tokens, norm_gain, w_in, taps, decay_rate, residues, skip_gain, w_out):
    T, D = tokens.shape[1:]
    C = w_in.shape[2]
    NP = decay_rate.shape[0]

    arrays, _ = scratch_of(nz, nctx, T, D, C, NP)
    dma = pltpu.SemaphoreType.DMA
    vmem, anywhere = pl.BlockSpec(memory_space=pltpu.VMEM), pl.BlockSpec(memory_space=pl.ANY)
    return pl.pallas_call(
        functools.partial(fused_kernel, nz, nctx),
        out_shape=jax.ShapeDtypeStruct((T, D), jnp.bfloat16),
        in_specs=[vmem, vmem, anywhere, vmem, vmem, vmem, vmem, anywhere],
        out_specs=vmem,
        scratch_shapes=[pltpu.VMEM(shape, kind) for shape, kind in arrays]
        + [
            dma((2,)),
            dma((3, 2 * nz, CHUNKS)),
            dma((2 * nz, CHUNKS)),
            dma((nz, CHUNKS)),
            dma((nz, CHUNKS)),
            dma((nz, CHUNKS)),
            dma((nz + 1, CHUNKS)),
            dma((nz,)),
            dma((nz + 1,)),
            dma((nz,)),
            dma((nz,)),
            dma((nz, nctx - 1)),
            dma((nz, nctx - 1)),
        ],
        compiler_params=pltpu.CompilerParams(
            collective_id=0, has_side_effects=True, vmem_limit_bytes=VMEM_LIMIT
        ),
    )(
        tokens[0], norm_gain[None], w_in.transpose(1, 0, 2), taps, decay_rate, residues, skip_gain[None], w_out,
    )[None]


def solution(mesh):
    in_specs = (
        P("fsdp", "ctx", None),
        P(),
        P(None, None, "fsdp"),
        P(None, None, "fsdp"),
        P(None, "fsdp"),
        P(None, "fsdp"),
        P("fsdp"),
        P("fsdp", None),
    )
    out_specs = P("fsdp", "ctx", None)
    count, nctx = mesh.shape["fsdp"], mesh.shape["ctx"]

    def whole(tokens, norm_gain, w_in, *rest):
        D, channels = w_in.shape[0], w_in.shape[2] // count
        length, poles = tokens.shape[1] // nctx, rest[1].shape[0]
        _, size = scratch_of(count // 2, nctx, length, D, channels, poles)
        fits = size <= VMEM_BUDGET and count % 2 == 0 and tokens.shape[0] == count
        fits = fits and channels % (4 * LANES) == 0 and length % (CHUNKS * STRIP) == 0
        chosen = functools.partial(fused_shards, count // 2, nctx) if fits else shards
        return sharded(chosen)(tokens, norm_gain, w_in, *rest)

    def sharded(body):
        return jax.shard_map(body, mesh=mesh, in_specs=in_specs, out_specs=out_specs, check_vma=False)

    return whole
```

```python
import functools

import jax
import jax.numpy as jnp
from jax import lax
from jax.experimental import pallas as pl
from jax.experimental.pallas import tpu as pltpu
from jax.sharding import PartitionSpec as P


def from_behind(value, axis, steps):
    count = lax.axis_size(axis)
    first, last = (max(0, -steps), min(count, count - steps))
    return lax.ppermute(value, axis, [(source, source + steps) for source in range(first, last)])


LANES = 128


def summary_kernel(decay_ref, product_ref, out_ref):
    poles, groups, lanes = out_ref.shape
    decay = jnp.broadcast_to(jnp.exp(-decay_ref[...])[:, None, :], (poles, groups, lanes))

    def step(t, state):
        return decay * state + product_ref[t][None]

    out_ref[...] = lax.fori_loop(0, product_ref.shape[0], step, jnp.zeros(out_ref.shape, jnp.float32))


def filter_kernel(decay_ref, residues_ref, skip_ref, product_ref, query_ref, incoming_ref, out_ref):
    poles, groups, lanes = incoming_ref.shape
    decay = jnp.broadcast_to(jnp.exp(-decay_ref[...])[:, None, :], (poles, groups, lanes))
    residues = residues_ref[...][:, None, :]
    skip = skip_ref[...]

    def step(t, state):
        product = product_ref[t]
        state = decay * state + product[None]
        out_ref[t] = query_ref[t] * (skip * product + jnp.sum(residues * state, axis=0))
        return state

    lax.fori_loop(0, product_ref.shape[0], step, incoming_ref[...])


def shards(tokens, norm_gain, w_in, taps, decay_rate, residues, skip_gain, w_out):
    values = tokens.astype(jnp.float32)
    inverse_rms = lax.rsqrt(jnp.mean(values * values, axis=-1, keepdims=True) + 1e-06)
    normed = (values * inverse_rms * norm_gain).astype(jnp.bfloat16)
    model_width = w_in.shape[0]
    channels = w_in.shape[2]
    w_flat = w_in.reshape(model_width, 3 * channels)
    features = jnp.einsum(
        "gtd,de->gte",
        lax.all_gather(normed, "fsdp", axis=0, tiled=True),
        w_flat,
        preferred_element_type=jnp.float32,
    ).astype(jnp.bfloat16)
    groups = features.shape[0]
    length = features.shape[1]
    poles = decay_rate.shape[0]
    edge_rows = from_behind(features[:, length - 2 :], "ctx", 1)
    extended = jnp.concatenate([edge_rows, features], axis=1).transpose(1, 0, 2).astype(jnp.float32)
    tap_rows = taps.reshape(taps.shape[0], 3 * channels)
    filtered = tap_rows[0] * extended[2:] + tap_rows[1] * extended[1:-1] + tap_rows[2] * extended[:-2]
    query_part = filtered[:, :, :channels]
    product = filtered[:, :, channels : 2 * channels] * filtered[:, :, 2 * channels :]
    pole_spec = pl.BlockSpec((poles, LANES), lambda c: (0, c))
    state_spec = pl.BlockSpec((poles, groups, LANES), lambda c: (0, 0, c))
    rows_spec = pl.BlockSpec((length, groups, LANES), lambda c: (0, 0, c))
    summary = pl.pallas_call(
        summary_kernel,
        grid=(channels // LANES,),
        in_specs=[pole_spec, rows_spec],
        out_specs=state_spec,
        out_shape=jax.ShapeDtypeStruct((poles, groups, channels), jnp.float32),
    )(decay_rate, product)
    decay_all = jnp.exp(-decay_rate * length)[:, None, :]
    incoming = jnp.zeros_like(summary)
    for hop_step in range(lax.axis_size("ctx") - 1):
        incoming = from_behind(
            (decay_all * incoming + summary).astype(jnp.bfloat16), "ctx", 1
        ).astype(jnp.float32)
    gated = pl.pallas_call(
        filter_kernel,
        grid=(channels // LANES,),
        in_specs=[pole_spec, pole_spec, pl.BlockSpec((1, LANES), lambda c: (0, c)), rows_spec, rows_spec, state_spec],
        out_specs=rows_spec,
        out_shape=jax.ShapeDtypeStruct((length, groups, channels), jnp.float32),
    )(decay_rate, residues, skip_gain[None], product, query_part, incoming)
    gated = gated.astype(jnp.bfloat16).transpose(1, 0, 2).reshape(groups * length, channels)
    summed = lax.psum_scatter(
        jnp.dot(gated, w_out, preferred_element_type=jnp.float32).astype(jnp.bfloat16),
        "fsdp",
        scatter_dimension=0,
        tiled=True,
    ).astype(jnp.float32)
    return (values[0] + summed).astype(jnp.bfloat16)[None]


CHUNKS = 8
ONCE = 2
LAG = 2
COLUMNS = 256
STRIP = 16
UNROLL = 4
VMEM_BUDGET = 52 * 1024 * 1024
VMEM_LIMIT = 63 * 1024 * 1024


def fused_kernel(
    nz, nctx,
    tok, gain, w_in, taps_in, decay_in, residues_in, skip_in, w_out,
    out,
    w_v, wo_v, gat, part, rxx, rz, feat, prod, query, gated, gated_rows, edge_rx, st_tx, st_rx, inc, acc, rzo,
    taps, decay, residues, skip, factor,
    w_sem, ag_send, ag_recv, x_send, x_recv, z_send, z_recv, o_send, o_recv, edge_send, edge_recv, st_send, st_recv,
):
    T, D = tok.shape
    C = w_in.shape[2]
    J = C // LANES
    R = 2 * J
    NP = decay_in.shape[0]
    TC = T // CHUNKS
    f = lax.axis_index("fsdp")
    c = lax.axis_index("ctx")
    z = lax.div(f, 2)
    x = lax.rem(f, 2)
    partner = z * 2 + 1 - x
    has_left, has_right = z > 0, z < nz - 1

    w_copy = pltpu.make_async_copy(w_in, w_v, w_sem.at[0])
    wo_copy = pltpu.make_async_copy(w_out, wo_v, w_sem.at[1])
    w_copy.start()
    wo_copy.start()

    barrier = pltpu.get_barrier_semaphore()
    pl.semaphore_signal(barrier, inc=1, device_id={"fsdp": partner}, device_id_type=pl.DeviceIdType.MESH)

    @pl.when(has_left)
    def _():
        pl.semaphore_signal(barrier, inc=1, device_id={"fsdp": f - 2}, device_id_type=pl.DeviceIdType.MESH)

    @pl.when(has_right)
    def _():
        pl.semaphore_signal(barrier, inc=1, device_id={"fsdp": f + 2}, device_id_type=pl.DeviceIdType.MESH)

    for d in range(1, nctx):
        pl.semaphore_signal(
            barrier, inc=1, device_id={"ctx": lax.rem(c + d, nctx)}, device_id_type=pl.DeviceIdType.MESH
        )

    def rows(start, size):
        return pl.ds(pl.multiple_of(start, STRIP), size)

    def remote(src, dst, send, recv, device):
        return pltpu.make_async_remote_copy(
            src_ref=src, dst_ref=dst, send_sem=send, recv_sem=recv,
            device_id=device, device_id_type=pl.DeviceIdType.MESH,
        )

    X, UP, DOWN = 0, 1, 2

    def ag(block, ch, way):
        where = gat.at[rows(block * T + ch * TC, TC), :]
        target = {X: partner, UP: f + 2, DOWN: f - 2}[way]
        return remote(
            where, where, ag_send.at[way, block, ch], ag_recv.at[block, ch], {"fsdp": target}
        )

    def part_x(p, ch):
        return remote(
            part.at[rows((p * 2 + 1 - x) * T + ch * TC, TC), :],
            rxx.at[rows(p * T + ch * TC, TC), :],
            x_send.at[p, ch], x_recv.at[p, ch], {"fsdp": partner},
        )

    def part_z(p, ch, slot, target):
        return remote(
            part.at[rows((p * 2 + x) * T + ch * TC, TC), :],
            rz.at[rows(slot * T + ch * TC, TC), :],
            z_send.at[p, ch], z_recv.at[slot, ch], {"fsdp": target},
        )

    for ch in range(CHUNKS):
        @pl.loop(ch * (TC // STRIP), (ch + 1) * (TC // STRIP))
        def _(k):
            value = tok[rows(k * STRIP, STRIP), :].astype(jnp.float32)
            scale = lax.rsqrt(jnp.mean(value * value, axis=-1, keepdims=True) + 1e-06)
            gat[rows(f * T + k * STRIP, STRIP), :] = (value * scale * gain[...]).astype(jnp.bfloat16)

        if ch == 0:
            pl.semaphore_wait(barrier, nctx + has_left.astype(jnp.int32) + has_right.astype(jnp.int32))
        ag(f, ch, X).start()

        @pl.when(has_right)
        def _():
            ag(f, ch, UP).start()

        @pl.when(has_left)
        def _():
            ag(f, ch, DOWN).start()

    for s in range(2):
        for j in range(J):
            row, lanes = s * J + j, slice(j * LANES, (j + 1) * LANES)
            for n in range(NP):
                decay[n, row : row + 1, :] = decay_in[n : n + 1, lanes]
                residues[n, row : row + 1, :] = residues_in[n : n + 1, lanes]
            for k in range(3):
                for i in range(3):
                    taps[k, i, row : row + 1, :] = taps_in[k, i : i + 1, lanes]
            skip[row : row + 1, :] = skip_in[0:1, lanes]
    factor[...] = jnp.exp(-decay[...])

    for ch in range(ONCE):
        ag(partner, ch, X).wait_recv()

        @pl.when(has_right)
        def _():
            ag(partner, ch, UP).start()

        @pl.when(has_left)
        def _():
            ag(partner, ch, DOWN).start()

    def compute(p):
        @pl.loop(ONCE, CHUNKS)
        def _(ch):
            ag(p * 2 + 1 - x, ch, X).wait_recv()

        for i in range(3):
            for n in range(C // COLUMNS):
                result = jnp.dot(
                    gat[rows(p * 2 * T, 2 * T), :],
                    w_v[i, :, n * COLUMNS : (n + 1) * COLUMNS],
                    preferred_element_type=jnp.float32,
                ).astype(jnp.bfloat16).astype(jnp.float32)
                for s in range(2):
                    for j in range(COLUMNS // LANES):
                        first = 2 * R + s * J + n * (COLUMNS // LANES) + j
                        feat[i, pl.ds(first, T, stride=R), :] = result[
                            s * T : (s + 1) * T, j * LANES : (j + 1) * LANES
                        ]

        edge = remote(
            feat.at[:, pl.ds(T * R, 2 * R), :], edge_rx.at[p], edge_send.at[p], edge_recv.at[p], {"ctx": c + 1}
        )

        @pl.when(c + 1 < nctx)
        def _():
            edge.start()

        def filter_row(base):
            filtered = [
                taps[0, i] * feat[i, pl.ds(pl.multiple_of(base + 2 * R, R), R), :]
                + taps[1, i] * feat[i, pl.ds(pl.multiple_of(base + R, R), R), :]
                + taps[2, i] * feat[i, pl.ds(pl.multiple_of(base, R), R), :]
                for i in range(3)
            ]
            product = filtered[1] * filtered[2]
            prod[pl.ds(pl.multiple_of(base, R), R), :] = product
            query[pl.ds(pl.multiple_of(base, R), R), :] = filtered[0]
            return product

        def first_pass(block, state):
            decays = [factor[n] for n in range(NP)]
            for k in range(UNROLL):
                base = (block * UNROLL + k) * R
                product = filter_row(base)
                state = tuple(decays[n] * state[n] + product for n in range(NP))
            return state

        state = (jnp.zeros((R, LANES), jnp.float32),) * NP
        for t in range(2, UNROLL):
            product = filter_row(t * R)
            state = tuple(factor[n] * state[n] + product for n in range(NP))
        state = lax.fori_loop(1, T // UNROLL, first_pass, state)
        for n in range(NP):
            inc[n] = state[n]

        @pl.when(c > 0)
        def _():
            edge.wait_recv()
            feat[:, 0 : 2 * R, :] = edge_rx[p]

        @pl.when(c == 0)
        def _():
            feat[:, 0 : 2 * R, :] = jnp.zeros((3, 2 * R, LANES), jnp.float32)

        early = [filter_row(t * R) for t in range(2)]
        for n in range(NP):
            inc[n] += (factor[n] * early[0] + early[1]) * jnp.exp(decay[n] * (-float(T - 2)))

        st_tx[p] = inc[...].reshape(NP * R, LANES).astype(jnp.bfloat16)

        def state_copy(d):
            return remote(
                st_tx.at[p], st_rx.at[p, d - 1], st_send.at[p, d - 1], st_recv.at[p, d - 1], {"ctx": c + d}
            )

        for d in range(1, nctx):
            @pl.when(c + d < nctx)
            def _():
                state_copy(d).start()

        inc[...] = jnp.zeros(inc.shape, jnp.float32)
        for d in range(1, nctx):
            @pl.when(c >= d)
            def _():
                state_copy(d).wait_recv()
                inc[...] += jnp.exp(decay[...] * (-float(T * (d - 1)))) * (
                    st_rx[p, d - 1].astype(jnp.float32).reshape(NP, R, LANES)
                )

        def second_pass(block, state):
            decays = [factor[n] for n in range(NP)]
            for k in range(UNROLL):
                here = pl.ds(pl.multiple_of((block * UNROLL + k) * R, R), R)
                product = prod[here, :]
                state = tuple(decays[n] * state[n] + product for n in range(NP))
                sums = [skip[...] * product] + [residues[n] * state[n] for n in range(NP)]
                while len(sums) > 1:
                    sums = [sum(sums[k : k + 2]) for k in range(0, len(sums), 2)]
                gated[here, :] = query[here, :] * sums[0]
            return state

        lax.fori_loop(0, T // UNROLL, second_pass, tuple(inc[n] for n in range(NP)))
        for s in range(2):
            for j in range(J):
                gated_rows[s * T : (s + 1) * T, j * LANES : (j + 1) * LANES] = gated[
                    pl.ds(s * J + j, T, stride=R), :
                ].astype(jnp.bfloat16)

        @pl.loop(0, D // COLUMNS)
        def _(n):
            where = pl.ds(pl.multiple_of(n * COLUMNS, COLUMNS), COLUMNS)
            part[rows(p * 2 * T, 2 * T), where] = jnp.dot(
                gated_rows[...], wo_v[:, where], preferred_element_type=jnp.float32
            ).astype(jnp.bfloat16)

        @pl.loop(ONCE, CHUNKS)
        def _(ch):
            part_x(p, ch).start()

        @pl.when(c + 1 < nctx)
        def _():
            edge.wait_send()

        for d in range(1, nctx):
            @pl.when(c + d < nctx)
            def _():
                state_copy(d).wait_send()

    w_copy.wait()
    wo_copy.wait()

    def main_step(h, carry):
        @pl.when(h < nz)
        def _():
            def relay(block, ch, way):
                ag(block, ch, way).wait_recv()

                @pl.when(has_right if way == UP else has_left)
                def _():
                    ag(block, ch, way).start()

            for column in range(2):
                @pl.loop(0, ONCE)
                def _(ch):
                    @pl.when(z - h >= 0)
                    def _():
                        relay((z - h) * 2 + column, ch, UP)

                    @pl.when(z + h < nz)
                    def _():
                        relay((z + h) * 2 + column, ch, DOWN)

            @pl.loop(ONCE, CHUNKS)
            def _(ch):
                @pl.when(z - h >= 0)
                def _():
                    block = (z - h) * 2 + x
                    relay(block, ch, UP)
                    ag(block, ch, X).start()

                @pl.when(z + h < nz)
                def _():
                    block = (z + h) * 2 + x
                    relay(block, ch, DOWN)
                    ag(block, ch, X).start()

        def side_step(side, carry):
            p = z + (h - 1) * (2 * side - 1)

            @pl.when((p >= 0) & (p < nz) & ((h > 1) | (side == 0)))
            def _():
                compute(p)

            return carry

        lax.fori_loop(0, 2, side_step, 0)

        @pl.when(h > 2)
        def _():
            reduce_step(h - 2)

        return carry

    def load(ref, start, k):
        return ref[rows(start + k * STRIP, STRIP), :].astype(jnp.float32)

    def combine(p, ch, more):
        start = (p * 2 + x) * T + ch * TC
        other = p * T + ch * TC
        part_x(p, ch).wait_recv()

        @pl.when(more)
        def _():
            part_z(p, ch, p, partner).wait_recv()

            @pl.loop(0, TC // STRIP)
            def _(k):
                total = load(part, start, k) + load(rxx, other, k) + load(rz, other, k)
                part[rows(start + k * STRIP, STRIP), :] = total.astype(jnp.bfloat16)

        @pl.when(jnp.logical_not(more))
        def _():
            @pl.loop(0, TC // STRIP)
            def _(k):
                total = load(part, start, k) + load(rxx, other, k)
                part[rows(start + k * STRIP, STRIP), :] = total.astype(jnp.bfloat16)

    def other_z(p, ch, slot, target):
        return remote(
            part.at[rows((p * 2 + 1 - x) * T + ch * TC, TC), :],
            rzo.at[rows((slot * ONCE + ch) * TC, TC), :],
            o_send.at[p, ch], o_recv.at[slot, ch], {"fsdp": target},
        )

    def add_in(start, ref, begin):
        @pl.loop(0, TC // STRIP)
        def _(k):
            total = load(part, start, k) + load(ref, begin, k)
            part[rows(start + k * STRIP, STRIP), :] = total.astype(jnp.bfloat16)

    def first_chunk(p, ch, more, slot, target):
        @pl.when(more)
        def _():
            part_z(p, ch, p, partner).wait_recv()
            add_in((p * 2 + x) * T + ch * TC, rz, p * T + ch * TC)

        part_z(p, ch, slot, target).start()

        @pl.when(more)
        def _():
            other_z(p, ch, p, partner).wait_recv()
            add_in((p * 2 + 1 - x) * T + ch * TC, rzo, (p * ONCE + ch) * TC)

        other_z(p, ch, slot, target).start()

    def send_sum(p, ch, more, slot, target):
        @pl.when(ch < ONCE)
        def _():
            first_chunk(p, ch, more, slot, target)

        @pl.when(ch >= ONCE)
        def _():
            combine(p, ch, more)
            part_z(p, ch, slot, target).start()

    up_late = (2 * z >= nz).astype(jnp.int32)

    def reduce_step(i):
        down = nz - 1 - i
        down_slot = jnp.where(down == z - 1, nz, down)

        @pl.loop(0, CHUNKS + LAG)
        def _(turn):
            up_ch, down_ch = turn - LAG * up_late, turn - LAG * (1 - up_late)

            @pl.when((i > z) & (up_ch >= 0) & (up_ch < CHUNKS))
            def _():
                send_sum(i, up_ch, has_left, i, f + 2)

            @pl.when((down < z) & (down_ch >= 0) & (down_ch < CHUNKS))
            def _():
                send_sum(down, down_ch, has_right, down_slot, f - 2)

    lax.fori_loop(1, nz + 1, main_step, 0)
    reduce_step(nz - 1)

    for ch in range(ONCE):
        for more, slot in ((has_left, z), (has_right, nz)):
            @pl.when(more)
            def _():
                other_z(z, ch, slot, partner).wait_recv()
                add_in(partner * T + ch * TC, rzo, (slot * ONCE + ch) * TC)

        part_x(z, ch).start()

    @pl.loop(0, CHUNKS)
    def _(turn):
        ch = lax.rem(turn + ONCE, CHUNKS)
        start = ch * TC
        part_x(z, ch).wait_recv()

        @pl.loop(0, TC // STRIP)
        def _(k):
            acc[rows(k * STRIP, STRIP), :] = (
                load(tok, start, k) + load(part, f * T + start, k) + load(rxx, z * T + start, k)
            )

        for more, slot in ((has_left, z), (has_right, nz)):
            @pl.when(more)
            def _():
                part_z(z, ch, slot, partner).wait_recv()

                @pl.loop(0, TC // STRIP)
                def _(k):
                    acc[rows(k * STRIP, STRIP), :] += load(rz, slot * T + start, k)

        @pl.loop(0, TC // STRIP)
        def _(k):
            out[rows(start + k * STRIP, STRIP), :] = acc[rows(k * STRIP, STRIP), :].astype(jnp.bfloat16)

    @pl.loop(0, nz)
    def _(p):
        @pl.loop(0, CHUNKS)
        def _(ch):
            @pl.when((ch >= ONCE) | (p == z))
            def _():
                ag(p * 2 + x, ch, X).wait_send()
                part_x(p, ch).wait_send()

            @pl.when((p <= z) & has_right)
            def _():
                ag(p * 2 + x, ch, UP).wait_send()

            @pl.when((p >= z) & has_left)
            def _():
                ag(p * 2 + x, ch, DOWN).wait_send()

            @pl.when(p != z)
            def _():
                part_z(p, ch, p, partner).wait_send()

        @pl.loop(0, ONCE)
        def _(ch):
            @pl.when((p <= z) & has_right)
            def _():
                ag(p * 2 + 1 - x, ch, UP).wait_send()

            @pl.when((p >= z) & has_left)
            def _():
                ag(p * 2 + 1 - x, ch, DOWN).wait_send()

            @pl.when(p != z)
            def _():
                other_z(p, ch, p, partner).wait_send()


def scratch_of(nz, nctx, T, D, C, NP):
    R = 2 * C // LANES
    f32, bf16 = jnp.float32, jnp.bfloat16
    arrays = [
        ((3, D, C), bf16),
        ((C, D), bf16),
        ((nz * 2 * T, D), bf16),
        ((nz * 2 * T, D), bf16),
        ((nz * T, D), bf16),
        (((nz + 1) * T, D), bf16),
        ((3, (T + 2) * R, LANES), f32),
        ((T * R, LANES), f32),
        ((T * R, LANES), f32),
        ((T * R, LANES), f32),
        ((2 * T, C), bf16),
        ((nz, 3, 2 * R, LANES), f32),
        ((nz, NP * R, LANES), bf16),
        ((nz, nctx - 1, NP * R, LANES), bf16),
        ((NP, R, LANES), f32),
        ((T // CHUNKS, D), f32),
        (((nz + 1) * ONCE * T // CHUNKS, D), bf16),
        ((3, 3, R, LANES), f32),
        ((NP, R, LANES), f32),
        ((NP, R, LANES), f32),
        ((R, LANES), f32),
        ((NP, R, LANES), f32),
    ]
    size = sum(functools.reduce(lambda a, b: a * b, shape) * jnp.dtype(kind).itemsize for shape, kind in arrays)
    return arrays, size


def fused_shards(nz, nctx, tokens, norm_gain, w_in, taps, decay_rate, residues, skip_gain, w_out):
    T, D = tokens.shape[1:]
    C = w_in.shape[2]
    NP = decay_rate.shape[0]

    arrays, _ = scratch_of(nz, nctx, T, D, C, NP)
    dma = pltpu.SemaphoreType.DMA
    vmem, anywhere = pl.BlockSpec(memory_space=pltpu.VMEM), pl.BlockSpec(memory_space=pl.ANY)
    return pl.pallas_call(
        functools.partial(fused_kernel, nz, nctx),
        out_shape=jax.ShapeDtypeStruct((T, D), jnp.bfloat16),
        in_specs=[vmem, vmem, anywhere, vmem, vmem, vmem, vmem, anywhere],
        out_specs=vmem,
        scratch_shapes=[pltpu.VMEM(shape, kind) for shape, kind in arrays]
        + [
            dma((2,)),
            dma((3, 2 * nz, CHUNKS)),
            dma((2 * nz, CHUNKS)),
            dma((nz, CHUNKS)),
            dma((nz, CHUNKS)),
            dma((nz, CHUNKS)),
            dma((nz + 1, CHUNKS)),
            dma((nz, ONCE)),
            dma((nz + 1, ONCE)),
            dma((nz,)),
            dma((nz,)),
            dma((nz, nctx - 1)),
            dma((nz, nctx - 1)),
        ],
        compiler_params=pltpu.CompilerParams(
            collective_id=0, has_side_effects=True, vmem_limit_bytes=VMEM_LIMIT
        ),
    )(
        tokens[0], norm_gain[None], w_in.transpose(1, 0, 2), taps, decay_rate, residues, skip_gain[None], w_out,
    )[None]


def solution(mesh):
    in_specs = (
        P("fsdp", "ctx", None),
        P(),
        P(None, None, "fsdp"),
        P(None, None, "fsdp"),
        P(None, "fsdp"),
        P(None, "fsdp"),
        P("fsdp"),
        P("fsdp", None),
    )
    out_specs = P("fsdp", "ctx", None)
    count, nctx = mesh.shape["fsdp"], mesh.shape["ctx"]

    def whole(tokens, norm_gain, w_in, *rest):
        D, channels = w_in.shape[0], w_in.shape[2] // count
        length, poles = tokens.shape[1] // nctx, rest[1].shape[0]
        _, size = scratch_of(count // 2, nctx, length, D, channels, poles)
        fits = size <= VMEM_BUDGET and count % 2 == 0 and tokens.shape[0] == count
        fits = fits and channels % (4 * LANES) == 0 and length % (CHUNKS * STRIP) == 0
        chosen = functools.partial(fused_shards, count // 2, nctx) if fits else shards
        return sharded(chosen)(tokens, norm_gain, w_in, *rest)

    def sharded(body):
        return jax.shard_map(body, mesh=mesh, in_specs=in_specs, out_specs=out_specs, check_vma=False)

    return whole
```

```python
import functools

import jax
import jax.numpy as jnp
from jax import lax
from jax.experimental import pallas as pl
from jax.experimental.pallas import tpu as pltpu
from jax.sharding import PartitionSpec as P


def from_behind(value, axis, steps):
    count = lax.axis_size(axis)
    first, last = (max(0, -steps), min(count, count - steps))
    return lax.ppermute(value, axis, [(source, source + steps) for source in range(first, last)])


LANES = 128


def summary_kernel(decay_ref, product_ref, out_ref):
    poles, groups, lanes = out_ref.shape
    decay = jnp.broadcast_to(jnp.exp(-decay_ref[...])[:, None, :], (poles, groups, lanes))

    def step(t, state):
        return decay * state + product_ref[t][None]

    out_ref[...] = lax.fori_loop(0, product_ref.shape[0], step, jnp.zeros(out_ref.shape, jnp.float32))


def filter_kernel(decay_ref, residues_ref, skip_ref, product_ref, query_ref, incoming_ref, out_ref):
    poles, groups, lanes = incoming_ref.shape
    decay = jnp.broadcast_to(jnp.exp(-decay_ref[...])[:, None, :], (poles, groups, lanes))
    residues = residues_ref[...][:, None, :]
    skip = skip_ref[...]

    def step(t, state):
        product = product_ref[t]
        state = decay * state + product[None]
        out_ref[t] = query_ref[t] * (skip * product + jnp.sum(residues * state, axis=0))
        return state

    lax.fori_loop(0, product_ref.shape[0], step, incoming_ref[...])


def shards(tokens, norm_gain, w_in, taps, decay_rate, residues, skip_gain, w_out):
    values = tokens.astype(jnp.float32)
    inverse_rms = lax.rsqrt(jnp.mean(values * values, axis=-1, keepdims=True) + 1e-06)
    normed = (values * inverse_rms * norm_gain).astype(jnp.bfloat16)
    model_width = w_in.shape[0]
    channels = w_in.shape[2]
    w_flat = w_in.reshape(model_width, 3 * channels)
    features = jnp.einsum(
        "gtd,de->gte",
        lax.all_gather(normed, "fsdp", axis=0, tiled=True),
        w_flat,
        preferred_element_type=jnp.float32,
    ).astype(jnp.bfloat16)
    groups = features.shape[0]
    length = features.shape[1]
    poles = decay_rate.shape[0]
    edge_rows = from_behind(features[:, length - 2 :], "ctx", 1)
    extended = jnp.concatenate([edge_rows, features], axis=1).transpose(1, 0, 2).astype(jnp.float32)
    tap_rows = taps.reshape(taps.shape[0], 3 * channels)
    filtered = tap_rows[0] * extended[2:] + tap_rows[1] * extended[1:-1] + tap_rows[2] * extended[:-2]
    query_part = filtered[:, :, :channels]
    product = filtered[:, :, channels : 2 * channels] * filtered[:, :, 2 * channels :]
    pole_spec = pl.BlockSpec((poles, LANES), lambda c: (0, c))
    state_spec = pl.BlockSpec((poles, groups, LANES), lambda c: (0, 0, c))
    rows_spec = pl.BlockSpec((length, groups, LANES), lambda c: (0, 0, c))
    summary = pl.pallas_call(
        summary_kernel,
        grid=(channels // LANES,),
        in_specs=[pole_spec, rows_spec],
        out_specs=state_spec,
        out_shape=jax.ShapeDtypeStruct((poles, groups, channels), jnp.float32),
    )(decay_rate, product)
    decay_all = jnp.exp(-decay_rate * length)[:, None, :]
    incoming = jnp.zeros_like(summary)
    for hop_step in range(lax.axis_size("ctx") - 1):
        incoming = from_behind(
            (decay_all * incoming + summary).astype(jnp.bfloat16), "ctx", 1
        ).astype(jnp.float32)
    gated = pl.pallas_call(
        filter_kernel,
        grid=(channels // LANES,),
        in_specs=[pole_spec, pole_spec, pl.BlockSpec((1, LANES), lambda c: (0, c)), rows_spec, rows_spec, state_spec],
        out_specs=rows_spec,
        out_shape=jax.ShapeDtypeStruct((length, groups, channels), jnp.float32),
    )(decay_rate, residues, skip_gain[None], product, query_part, incoming)
    gated = gated.astype(jnp.bfloat16).transpose(1, 0, 2).reshape(groups * length, channels)
    summed = lax.psum_scatter(
        jnp.dot(gated, w_out, preferred_element_type=jnp.float32).astype(jnp.bfloat16),
        "fsdp",
        scatter_dimension=0,
        tiled=True,
    ).astype(jnp.float32)
    return (values[0] + summed).astype(jnp.bfloat16)[None]


CHUNKS = 8
ONCE = 2
LAG = 2
COLUMNS = 256
STRIP = 16
UNROLL = 4
VMEM_BUDGET = 52 * 1024 * 1024
VMEM_LIMIT = 63 * 1024 * 1024


def fused_kernel(
    nz, nctx,
    tok, gain, w_in, taps_in, decay_in, residues_in, skip_in, w_out,
    out,
    w_v, wo_v, gat, part, rxx, rz, feat, prod, query, gated, gated_rows, edge_rx, st_tx, st_rx, inc, acc, rzo,
    taps, decay, residues, skip, factor,
    w_sem, ag_send, ag_recv, x_send, x_recv, z_send, z_recv, o_send, o_recv, edge_send, edge_recv, st_send, st_recv,
):
    T, D = tok.shape
    C = w_in.shape[2]
    J = C // LANES
    R = 2 * J
    NP = decay_in.shape[0]
    TC = T // CHUNKS
    f = lax.axis_index("fsdp")
    c = lax.axis_index("ctx")
    z = lax.div(f, 2)
    x = lax.rem(f, 2)
    partner = z * 2 + 1 - x
    has_left, has_right = z > 0, z < nz - 1

    w_copy = pltpu.make_async_copy(w_in, w_v, w_sem.at[0])
    wo_copy = pltpu.make_async_copy(w_out, wo_v, w_sem.at[1])
    w_copy.start()
    wo_copy.start()

    barrier = pltpu.get_barrier_semaphore()
    pl.semaphore_signal(barrier, inc=1, device_id={"fsdp": partner}, device_id_type=pl.DeviceIdType.MESH)

    @pl.when(has_left)
    def _():
        pl.semaphore_signal(barrier, inc=1, device_id={"fsdp": f - 2}, device_id_type=pl.DeviceIdType.MESH)

    @pl.when(has_right)
    def _():
        pl.semaphore_signal(barrier, inc=1, device_id={"fsdp": f + 2}, device_id_type=pl.DeviceIdType.MESH)

    for d in range(1, nctx):
        pl.semaphore_signal(
            barrier, inc=1, device_id={"ctx": lax.rem(c + d, nctx)}, device_id_type=pl.DeviceIdType.MESH
        )

    def rows(start, size):
        return pl.ds(pl.multiple_of(start, STRIP), size)

    def remote(src, dst, send, recv, device):
        return pltpu.make_async_remote_copy(
            src_ref=src, dst_ref=dst, send_sem=send, recv_sem=recv,
            device_id=device, device_id_type=pl.DeviceIdType.MESH,
        )

    X, UP, DOWN = 0, 1, 2

    def ag(block, ch, way):
        where = gat.at[rows(block * T + ch * TC, TC), :]
        target = {X: partner, UP: f + 2, DOWN: f - 2}[way]
        return remote(
            where, where, ag_send.at[way, block, ch], ag_recv.at[block, ch], {"fsdp": target}
        )

    def part_x(p, ch):
        return remote(
            part.at[rows((p * 2 + 1 - x) * T + ch * TC, TC), :],
            rxx.at[rows(p * T + ch * TC, TC), :],
            x_send.at[p, ch], x_recv.at[p, ch], {"fsdp": partner},
        )

    def part_z(p, ch, slot, target):
        return remote(
            part.at[rows((p * 2 + x) * T + ch * TC, TC), :],
            rz.at[rows(slot * T + ch * TC, TC), :],
            z_send.at[p, ch], z_recv.at[slot, ch], {"fsdp": target},
        )

    for ch in range(CHUNKS):
        @pl.loop(ch * (TC // STRIP), (ch + 1) * (TC // STRIP))
        def _(k):
            value = tok[rows(k * STRIP, STRIP), :].astype(jnp.float32)
            scale = lax.rsqrt(jnp.mean(value * value, axis=-1, keepdims=True) + 1e-06)
            gat[rows(f * T + k * STRIP, STRIP), :] = (value * scale * gain[...]).astype(jnp.bfloat16)

        if ch == 0:
            pl.semaphore_wait(barrier, nctx + has_left.astype(jnp.int32) + has_right.astype(jnp.int32))
        ag(f, ch, X).start()

        @pl.when(has_right)
        def _():
            ag(f, ch, UP).start()

        @pl.when(has_left)
        def _():
            ag(f, ch, DOWN).start()

    for s in range(2):
        for j in range(J):
            row, lanes = s * J + j, slice(j * LANES, (j + 1) * LANES)
            for n in range(NP):
                decay[n, row : row + 1, :] = decay_in[n : n + 1, lanes]
                residues[n, row : row + 1, :] = residues_in[n : n + 1, lanes]
            for k in range(3):
                for i in range(3):
                    taps[k, i, row : row + 1, :] = taps_in[k, i : i + 1, lanes]
            skip[row : row + 1, :] = skip_in[0:1, lanes]
    factor[...] = jnp.exp(-decay[...])

    for ch in range(ONCE):
        ag(partner, ch, X).wait_recv()

        @pl.when(has_right)
        def _():
            ag(partner, ch, UP).start()

        @pl.when(has_left)
        def _():
            ag(partner, ch, DOWN).start()

    def compute(p, meanwhile):
        @pl.loop(ONCE, CHUNKS)
        def _(ch):
            ag(p * 2 + 1 - x, ch, X).wait_recv()

        for i in range(3):
            for n in range(C // COLUMNS):
                result = jnp.dot(
                    gat[rows(p * 2 * T, 2 * T), :],
                    w_v[i, :, n * COLUMNS : (n + 1) * COLUMNS],
                    preferred_element_type=jnp.float32,
                ).astype(jnp.bfloat16).astype(jnp.float32)
                for s in range(2):
                    for j in range(COLUMNS // LANES):
                        first = 2 * R + s * J + n * (COLUMNS // LANES) + j
                        feat[i, pl.ds(first, T, stride=R), :] = result[
                            s * T : (s + 1) * T, j * LANES : (j + 1) * LANES
                        ]

        edge = remote(
            feat.at[:, pl.ds(T * R, 2 * R), :], edge_rx.at[p], edge_send.at[p], edge_recv.at[p], {"ctx": c + 1}
        )

        @pl.when(c + 1 < nctx)
        def _():
            edge.start()

        def filter_row(base):
            filtered = [
                taps[0, i] * feat[i, pl.ds(pl.multiple_of(base + 2 * R, R), R), :]
                + taps[1, i] * feat[i, pl.ds(pl.multiple_of(base + R, R), R), :]
                + taps[2, i] * feat[i, pl.ds(pl.multiple_of(base, R), R), :]
                for i in range(3)
            ]
            product = filtered[1] * filtered[2]
            prod[pl.ds(pl.multiple_of(base, R), R), :] = product
            query[pl.ds(pl.multiple_of(base, R), R), :] = filtered[0]
            return product

        def first_pass(block, state):
            decays = [factor[n] for n in range(NP)]
            for k in range(UNROLL):
                base = (block * UNROLL + k) * R
                product = filter_row(base)
                state = tuple(decays[n] * state[n] + product for n in range(NP))
            return state

        state = (jnp.zeros((R, LANES), jnp.float32),) * NP
        for t in range(2, UNROLL):
            product = filter_row(t * R)
            state = tuple(factor[n] * state[n] + product for n in range(NP))
        state = lax.fori_loop(1, T // UNROLL, first_pass, state)
        for n in range(NP):
            inc[n] = state[n]

        @pl.when(c > 0)
        def _():
            edge.wait_recv()
            feat[:, 0 : 2 * R, :] = edge_rx[p]

        @pl.when(c == 0)
        def _():
            feat[:, 0 : 2 * R, :] = jnp.zeros((3, 2 * R, LANES), jnp.float32)

        early = [filter_row(t * R) for t in range(2)]
        for n in range(NP):
            inc[n] += (factor[n] * early[0] + early[1]) * jnp.exp(decay[n] * (-float(T - 2)))

        st_tx[p] = inc[...].reshape(NP * R, LANES).astype(jnp.bfloat16)

        def state_copy(d):
            return remote(
                st_tx.at[p], st_rx.at[p, d - 1], st_send.at[p, d - 1], st_recv.at[p, d - 1], {"ctx": c + d}
            )

        for d in range(1, nctx):
            @pl.when(c + d < nctx)
            def _():
                state_copy(d).start()

        meanwhile()
        inc[...] = jnp.zeros(inc.shape, jnp.float32)
        for d in range(1, nctx):
            @pl.when(c >= d)
            def _():
                state_copy(d).wait_recv()
                inc[...] += jnp.exp(decay[...] * (-float(T * (d - 1)))) * (
                    st_rx[p, d - 1].astype(jnp.float32).reshape(NP, R, LANES)
                )

        def second_pass(block, state):
            decays = [factor[n] for n in range(NP)]
            for k in range(UNROLL):
                here = pl.ds(pl.multiple_of((block * UNROLL + k) * R, R), R)
                product = prod[here, :]
                state = tuple(decays[n] * state[n] + product for n in range(NP))
                sums = [skip[...] * product] + [residues[n] * state[n] for n in range(NP)]
                while len(sums) > 1:
                    sums = [sum(sums[k : k + 2]) for k in range(0, len(sums), 2)]
                gated[here, :] = query[here, :] * sums[0]
            return state

        lax.fori_loop(0, T // UNROLL, second_pass, tuple(inc[n] for n in range(NP)))
        for s in range(2):
            for j in range(J):
                gated_rows[s * T : (s + 1) * T, j * LANES : (j + 1) * LANES] = gated[
                    pl.ds(s * J + j, T, stride=R), :
                ].astype(jnp.bfloat16)

        @pl.loop(0, D // COLUMNS)
        def _(n):
            where = pl.ds(pl.multiple_of(n * COLUMNS, COLUMNS), COLUMNS)
            part[rows(p * 2 * T, 2 * T), where] = jnp.dot(
                gated_rows[...], wo_v[:, where], preferred_element_type=jnp.float32
            ).astype(jnp.bfloat16)

        @pl.when(p != z)
        def _():
            @pl.loop(ONCE, CHUNKS)
            def _(ch):
                part_x(p, ch).start()

        @pl.when(c + 1 < nctx)
        def _():
            edge.wait_send()

        for d in range(1, nctx):
            @pl.when(c + d < nctx)
            def _():
                state_copy(d).wait_send()

    w_copy.wait()
    wo_copy.wait()

    def main_step(h, carry):
        @pl.when(h < nz)
        def _():
            def relay(block, ch, way):
                ag(block, ch, way).wait_recv()

                @pl.when(has_right if way == UP else has_left)
                def _():
                    ag(block, ch, way).start()

            for column in range(2):
                @pl.loop(0, ONCE)
                def _(ch):
                    @pl.when(z - h >= 0)
                    def _():
                        relay((z - h) * 2 + column, ch, UP)

                    @pl.when(z + h < nz)
                    def _():
                        relay((z + h) * 2 + column, ch, DOWN)

            @pl.loop(ONCE, CHUNKS)
            def _(ch):
                @pl.when(z - h >= 0)
                def _():
                    block = (z - h) * 2 + x
                    relay(block, ch, UP)
                    ag(block, ch, X).start()

                @pl.when(z + h < nz)
                def _():
                    block = (z + h) * 2 + x
                    relay(block, ch, DOWN)
                    ag(block, ch, X).start()

        def meanwhile():
            @pl.when(h > 2)
            def _():
                reduce_step(h - 2, jnp.logical_not(has_left), jnp.logical_not(has_right))

        def side_step(side, carry):
            p = z + (h - 1) * (2 * side - 1)

            @pl.when((p >= 0) & (p < nz) & ((h > 1) | (side == 0)))
            def _():
                compute(p, meanwhile)

            return carry

        lax.fori_loop(0, 2, side_step, 0)

        @pl.when(h > 2)
        def _():
            reduce_step(h - 2, has_left, has_right)

        return carry

    def load(ref, start, k):
        return ref[rows(start + k * STRIP, STRIP), :].astype(jnp.float32)

    def combine(p, ch, more):
        start = (p * 2 + x) * T + ch * TC
        other = p * T + ch * TC
        part_x(p, ch).wait_recv()

        @pl.when(more)
        def _():
            part_z(p, ch, p, partner).wait_recv()

            @pl.loop(0, TC // STRIP)
            def _(k):
                total = load(part, start, k) + load(rxx, other, k) + load(rz, other, k)
                part[rows(start + k * STRIP, STRIP), :] = total.astype(jnp.bfloat16)

        @pl.when(jnp.logical_not(more))
        def _():
            @pl.loop(0, TC // STRIP)
            def _(k):
                total = load(part, start, k) + load(rxx, other, k)
                part[rows(start + k * STRIP, STRIP), :] = total.astype(jnp.bfloat16)

    def other_z(p, ch, slot, target):
        return remote(
            part.at[rows((p * 2 + 1 - x) * T + ch * TC, TC), :],
            rzo.at[rows((slot * ONCE + ch) * TC, TC), :],
            o_send.at[p, ch], o_recv.at[slot, ch], {"fsdp": target},
        )

    def add_in(start, ref, begin):
        @pl.loop(0, TC // STRIP)
        def _(k):
            total = load(part, start, k) + load(ref, begin, k)
            part[rows(start + k * STRIP, STRIP), :] = total.astype(jnp.bfloat16)

    def first_chunk(p, ch, more, slot, target):
        @pl.when(more)
        def _():
            part_z(p, ch, p, partner).wait_recv()
            add_in((p * 2 + x) * T + ch * TC, rz, p * T + ch * TC)

        part_z(p, ch, slot, target).start()

        @pl.when(more)
        def _():
            other_z(p, ch, p, partner).wait_recv()
            add_in((p * 2 + 1 - x) * T + ch * TC, rzo, (p * ONCE + ch) * TC)

        other_z(p, ch, slot, target).start()

    def send_sum(p, ch, more, slot, target):
        @pl.when(ch < ONCE)
        def _():
            first_chunk(p, ch, more, slot, target)

        @pl.when(ch >= ONCE)
        def _():
            combine(p, ch, more)
            part_z(p, ch, slot, target).start()

    up_late = (2 * z >= nz).astype(jnp.int32)

    def reduce_step(i, ups, downs):
        down = nz - 1 - i
        down_slot = jnp.where(down == z - 1, nz, down)

        @pl.loop(0, CHUNKS + LAG)
        def _(turn):
            up_ch, down_ch = turn - LAG * up_late, turn - LAG * (1 - up_late)

            @pl.when(ups & (i > z) & (up_ch >= 0) & (up_ch < CHUNKS))
            def _():
                send_sum(i, up_ch, has_left, i, f + 2)

            @pl.when(downs & (down < z) & (down_ch >= 0) & (down_ch < CHUNKS))
            def _():
                send_sum(down, down_ch, has_right, down_slot, f - 2)

    lax.fori_loop(1, nz + 1, main_step, 0)

    @pl.loop(ONCE, CHUNKS)
    def _(ch):
        part_x(z, ch).start()

    reduce_step(nz - 1, True, True)

    for ch in range(ONCE):
        for more, slot in ((has_left, z), (has_right, nz)):
            @pl.when(more)
            def _():
                other_z(z, ch, slot, partner).wait_recv()
                add_in(partner * T + ch * TC, rzo, (slot * ONCE + ch) * TC)

        part_x(z, ch).start()

    @pl.loop(0, CHUNKS)
    def _(turn):
        ch = lax.rem(turn + ONCE, CHUNKS)
        start = ch * TC
        part_x(z, ch).wait_recv()

        @pl.loop(0, TC // STRIP)
        def _(k):
            acc[rows(k * STRIP, STRIP), :] = (
                load(tok, start, k) + load(part, f * T + start, k) + load(rxx, z * T + start, k)
            )

        for more, slot in ((has_left, z), (has_right, nz)):
            @pl.when(more)
            def _():
                part_z(z, ch, slot, partner).wait_recv()

                @pl.loop(0, TC // STRIP)
                def _(k):
                    acc[rows(k * STRIP, STRIP), :] += load(rz, slot * T + start, k)

        @pl.loop(0, TC // STRIP)
        def _(k):
            out[rows(start + k * STRIP, STRIP), :] = acc[rows(k * STRIP, STRIP), :].astype(jnp.bfloat16)

    @pl.loop(0, nz)
    def _(p):
        @pl.loop(0, CHUNKS)
        def _(ch):
            @pl.when((ch >= ONCE) | (p == z))
            def _():
                ag(p * 2 + x, ch, X).wait_send()
                part_x(p, ch).wait_send()

            @pl.when((p <= z) & has_right)
            def _():
                ag(p * 2 + x, ch, UP).wait_send()

            @pl.when((p >= z) & has_left)
            def _():
                ag(p * 2 + x, ch, DOWN).wait_send()

            @pl.when(p != z)
            def _():
                part_z(p, ch, p, partner).wait_send()

        @pl.loop(0, ONCE)
        def _(ch):
            @pl.when((p <= z) & has_right)
            def _():
                ag(p * 2 + 1 - x, ch, UP).wait_send()

            @pl.when((p >= z) & has_left)
            def _():
                ag(p * 2 + 1 - x, ch, DOWN).wait_send()

            @pl.when(p != z)
            def _():
                other_z(p, ch, p, partner).wait_send()


def scratch_of(nz, nctx, T, D, C, NP):
    R = 2 * C // LANES
    f32, bf16 = jnp.float32, jnp.bfloat16
    arrays = [
        ((3, D, C), bf16),
        ((C, D), bf16),
        ((nz * 2 * T, D), bf16),
        ((nz * 2 * T, D), bf16),
        ((nz * T, D), bf16),
        (((nz + 1) * T, D), bf16),
        ((3, (T + 2) * R, LANES), f32),
        ((T * R, LANES), f32),
        ((T * R, LANES), f32),
        ((T * R, LANES), f32),
        ((2 * T, C), bf16),
        ((nz, 3, 2 * R, LANES), f32),
        ((nz, NP * R, LANES), bf16),
        ((nz, nctx - 1, NP * R, LANES), bf16),
        ((NP, R, LANES), f32),
        ((T // CHUNKS, D), f32),
        (((nz + 1) * ONCE * T // CHUNKS, D), bf16),
        ((3, 3, R, LANES), f32),
        ((NP, R, LANES), f32),
        ((NP, R, LANES), f32),
        ((R, LANES), f32),
        ((NP, R, LANES), f32),
    ]
    size = sum(functools.reduce(lambda a, b: a * b, shape) * jnp.dtype(kind).itemsize for shape, kind in arrays)
    return arrays, size


def fused_shards(nz, nctx, tokens, norm_gain, w_in, taps, decay_rate, residues, skip_gain, w_out):
    T, D = tokens.shape[1:]
    C = w_in.shape[2]
    NP = decay_rate.shape[0]

    arrays, _ = scratch_of(nz, nctx, T, D, C, NP)
    dma = pltpu.SemaphoreType.DMA
    vmem, anywhere = pl.BlockSpec(memory_space=pltpu.VMEM), pl.BlockSpec(memory_space=pl.ANY)
    return pl.pallas_call(
        functools.partial(fused_kernel, nz, nctx),
        out_shape=jax.ShapeDtypeStruct((T, D), jnp.bfloat16),
        in_specs=[vmem, vmem, anywhere, vmem, vmem, vmem, vmem, anywhere],
        out_specs=vmem,
        scratch_shapes=[pltpu.VMEM(shape, kind) for shape, kind in arrays]
        + [
            dma((2,)),
            dma((3, 2 * nz, CHUNKS)),
            dma((2 * nz, CHUNKS)),
            dma((nz, CHUNKS)),
            dma((nz, CHUNKS)),
            dma((nz, CHUNKS)),
            dma((nz + 1, CHUNKS)),
            dma((nz, ONCE)),
            dma((nz + 1, ONCE)),
            dma((nz,)),
            dma((nz,)),
            dma((nz, nctx - 1)),
            dma((nz, nctx - 1)),
        ],
        compiler_params=pltpu.CompilerParams(
            collective_id=0, has_side_effects=True, vmem_limit_bytes=VMEM_LIMIT
        ),
    )(
        tokens[0], norm_gain[None], w_in.transpose(1, 0, 2), taps, decay_rate, residues, skip_gain[None], w_out,
    )[None]


def solution(mesh):
    in_specs = (
        P("fsdp", "ctx", None),
        P(),
        P(None, None, "fsdp"),
        P(None, None, "fsdp"),
        P(None, "fsdp"),
        P(None, "fsdp"),
        P("fsdp"),
        P("fsdp", None),
    )
    out_specs = P("fsdp", "ctx", None)
    count, nctx = mesh.shape["fsdp"], mesh.shape["ctx"]

    def whole(tokens, norm_gain, w_in, *rest):
        D, channels = w_in.shape[0], w_in.shape[2] // count
        length, poles = tokens.shape[1] // nctx, rest[1].shape[0]
        _, size = scratch_of(count // 2, nctx, length, D, channels, poles)
        fits = size <= VMEM_BUDGET and count % 2 == 0 and tokens.shape[0] == count
        fits = fits and channels % (4 * LANES) == 0 and length % (CHUNKS * STRIP) == 0
        chosen = functools.partial(fused_shards, count // 2, nctx) if fits else shards
        return sharded(chosen)(tokens, norm_gain, w_in, *rest)

    def sharded(body):
        return jax.shard_map(body, mesh=mesh, in_specs=in_specs, out_specs=out_specs, check_vma=False)

    return whole
```
